256 devices in a mesh: layer: 16 (over z, x_hi), dp: 16 (over x_lo, y, core).
Axes of the slice: x: 4 (x_hi: 2, x_lo: 2; x = x_hi * 2 + x_lo), y: 4, z: 8, core: 2. Of those that a mesh axis runs over, the one named last changes fastest.
Arguments:
- query_grads: float32 [16, 1024, 4096], P('layer', 'dp'), may hold values from -6 to 6
- train_grads: float32 [16, 4096, 4096], P('layer', 'dp'), may hold values from -6 to 6
- eig_out: float32 [16, 64, 64], P('layer'), may hold values from -0.75 to 0.75
- eig_in: float32 [16, 64, 64], P('layer'), may hold values from -0.75 to 0.75
- eig_values: float32 [16, 4096], P('layer'), may hold values from 0.05 to 5
- train_ids: int32 [4096], P('dp'), may hold values from 0 to 9999999
Outputs:
- influence: float32 [1024, 4096], P('layer', 'dp')
The draws below stay inside these ranges and needn't reach their ends.
All inputs are finite; a program needn't handle non-finite values.
Results may differ from the reference program's by a relative error of at most 0.0001.
Values sent between devices are 32-bit elements; how exact they have to be, the bound alone decides.
A program may use at most 192 MiB of HBM per device.

```python
import math
import jax
import jax.numpy as jnp
from jax import lax

R = 64
C = 64
CORPUS = 10000000
LAYERS = 16
NQ = 1024
NTRAIN = 4096


def place_ends(values, own_key, least, top_value):
    dims = values.shape
    place = [jax.random.randint(jax.random.fold_in(own_key, axis), (), 0, dims[axis]) for axis in range(len(dims))]
    values = values.at[tuple(place)].set(least)
    longest = dims.index(max(dims))
    place[longest] = (place[longest] + 1) % dims[longest]
    return values.at[tuple(place)].set(top_value)


def spiked(drawn, own_key, source, target, parts, factor):
    def block_of(dim):
        return (jnp.arange(drawn.shape[dim]) // (drawn.shape[dim] // parts)).reshape((-1,) + (1,) * (drawn.ndim - 1 - dim))

    near = jax.random.permutation(own_key, parts)[block_of(target)]
    other_side = (block_of(target) + parts // 2) % parts
    return jnp.where((block_of(source) == near) | (block_of(source) == other_side), factor * drawn, drawn)


def shard_levels(stream_key, shape, cuts, smallest, high):
    loudness = 1.0
    for axis_at, parts in cuts:
        heights = jax.random.uniform(jax.random.fold_in(jax.random.fold_in(stream_key, 6), axis_at), (parts,), jnp.float32, smallest / len(cuts), high / len(cuts))
        loudness = loudness * jnp.repeat(jnp.exp(heights), shape[axis_at] // parts).reshape((-1,) + (1,) * (len(shape) - 1 - axis_at))
    return loudness


def bell_draw(stream_key, shape, spread, reach, pieces=(), held_as=jnp.bfloat16):
    array = spread * jax.random.normal(stream_key, shape, jnp.float32)
    if pieces:
        array = array * shard_levels(stream_key, shape, pieces, -0.22, 0.18)
    return jnp.clip(array, -reach, reach).astype(held_as)


def heavy_noise(stream_key, extent, spread, bound, split, heavy, kind=jnp.bfloat16):
    entries = spread * jax.random.normal(stream_key, extent, jnp.float32)
    if split:
        entries = entries * shard_levels(stream_key, extent, split, -0.22, 0.18)
    return jnp.clip(spiked(entries, jax.random.fold_in(stream_key, 3), *heavy), -bound, bound).astype(kind)


def setup_inputs(seed: int = 0) -> dict:
    key_list = jax.random.split(jax.random.key(seed), 7)
    return {
        "query_grads": heavy_noise(key_list[0], (LAYERS, NQ, R * C), 1.0, 6.0, ((0, 16), (1, 16)), (0, 1, 16, 2.0), jnp.float32),
        "train_grads": bell_draw(key_list[1], (LAYERS, NTRAIN, R * C), 1.0, 6.0, ((0, 16), (1, 16)), jnp.float32),
        "eig_out": bell_draw(key_list[2], (LAYERS, R, R), R ** -0.5, 0.75, ((0, 16),), jnp.float32),
        "eig_in": bell_draw(key_list[3], (LAYERS, C, C), C ** -0.5, 0.75, ((0, 16),), jnp.float32),
        "eig_values": jnp.clip(jnp.exp(math.log(5.0) - 4.6051702 * jax.random.uniform(key_list[4], (LAYERS, R * C), jnp.float32) ** shard_levels(key_list[4], (LAYERS, R * C), ((0, 16),), -0.2, 0.2)), 0.05, 5.0),
        "train_ids": place_ends(jax.random.randint(key_list[5], (NTRAIN,), 0, CORPUS), jax.random.fold_in(key_list[5], 1), 0, CORPUS - 1).astype(jnp.int32),
    }


def rotate(grads, eig_out, eig_in):
    count = grads.shape[0]
    shaped = grads.reshape(count, R, C)
    turned = jnp.einsum('nrc,rs->nsc', shaped, eig_out, precision=lax.Precision.HIGHEST)
    turned = jnp.einsum('nsc,ct->nst', turned, eig_in, precision=lax.Precision.HIGHEST)
    return turned.reshape(count, R * C)

def reference(query_grads, train_grads, eig_out, eig_in, eig_values, train_ids):

    def one_layer(total, inputs):
        query_layer, train_layer, out_basis, in_basis, values = inputs
        damping = 0.1 * jnp.mean(values)
        damped_inverse = 1.0 / (values + damping)
        query_side = rotate(query_layer, out_basis, in_basis) * damped_inverse[None, :]
        train_side = rotate(train_layer, out_basis, in_basis)
        total = total + jnp.dot(query_side, train_side.T, precision=lax.Precision.HIGHEST, preferred_element_type=jnp.float32)
        return (total, None)
    start_total = jnp.zeros((query_grads.shape[1], train_grads.shape[1]), jnp.float32)
    total, unused = lax.scan(one_layer, start_total, (query_grads, train_grads, eig_out, eig_in, eig_values))
    position = train_ids.astype(jnp.float32) / float(CORPUS)
    rate = 0.1 + 0.45 * (1.0 + jnp.cos(jnp.pi * position))
    return total * rate[None, :] / math.sqrt(float(R * C * LAYERS))
```

```python
import functools
import math

import jax
import jax.numpy as jnp
from jax import lax
from jax.experimental import pallas as pl
from jax.experimental.pallas import tpu as pltpu
from jax.sharding import PartitionSpec as P

CORPUS = 10000000
MESH = pl.DeviceIdType.MESH
PIECES = 4

STEPS = ((0, 0), (0, 1), (0, -1), (1, 0), (0, 2), (1, 1), (1, -1), (1, 2))


def split(value):
    high = value.astype(jnp.bfloat16)
    low = (value - high.astype(jnp.float32)).astype(jnp.bfloat16)
    return high, low


def kernel(q_ref, t_ref, o_ref, held, t_land, t_hi, t_lo, q_hi, q_lo, scores, landed,
           load_sem, t_sem, send_sem, half_sem, recv_sem, out_sem, in_sem):
    layer = lax.axis_index("layer")
    dp = lax.axis_index("dp")
    core, y, x = dp % 2, (dp // 2) % 4, dp // 8
    count = q_ref.shape[0]
    rows = count // PIECES
    half = rows // 2
    layers = landed.shape[0]

    def place(dx, dy, dc):
        return (((x + dx) % 2) * 4 + (y + dy + 4) % 4) * 2 + (core + dc) % 2

    x_flip, y_up, y_down, twin = place(1, 0, 0), place(0, 1, 0), place(0, -1, 0), place(0, 0, 1)

    barrier = pltpu.get_barrier_semaphore()
    for other in (x_flip, y_up, y_down, twin):
        pl.semaphore_signal(barrier, inc=1, device_id={"dp": other}, device_id_type=MESH)

    @pl.loop(1, layers)
    def _(step):
        pl.semaphore_signal(barrier, inc=1, device_id={"layer": (layer + step) % layers}, device_id_type=MESH)

    own = pltpu.make_async_copy(q_ref, held.at[0], load_sem)
    own.start()
    t_load = pltpu.make_async_copy(t_ref, t_land, t_sem)
    t_load.start()
    own.wait()
    pl.semaphore_wait(barrier, 4 + layers - 1)

    def send(slot, piece, target, to_slot, kind, first=0, size=None, from_sem=None, arrival=None):
        size = rows if size is None else size
        window = pl.ds(pl.multiple_of(piece * rows + first, 8), size)
        pltpu.make_async_remote_copy(
            src_ref=held.at[slot, window, :],
            dst_ref=held.at[to_slot, window, :],
            send_sem=send_sem.at[kind] if from_sem is None else from_sem,
            recv_sem=recv_sem.at[to_slot if arrival is None else arrival, piece],
            device_id={"dp": target},
            device_id_type=MESH,
        ).start()

    def arrive(slot, piece, first=0, size=None, arrival=None):
        size = rows if size is None else size
        window = pl.ds(pl.multiple_of(piece * rows + first, 8), size)
        block = held.at[slot, window, :]
        pltpu.make_async_copy(block, block, recv_sem.at[slot if arrival is None else arrival, piece]).wait()

    @pl.loop(0, PIECES)
    def _(piece):
        send(0, piece, y_up, 1, 0)
        send(0, piece, y_down, 2, 1)
        send(0, piece, x_flip, 3, 2)
        send(0, piece, twin, 8, 8)

    t_load.wait()
    tiles = 16
    t_rows = t_ref.shape[0] // tiles

    @pl.loop(0, tiles)
    def _(tile):
        window = pl.ds(pl.multiple_of(tile * t_rows, 16), t_rows)
        t_hi[window, :], t_lo[window, :] = split(t_land[window, :])

    def relay_near(piece):
        arrive(1, piece)
        send(1, piece, y_up, 4, None, 0, half, half_sem.at[0])
        send(1, piece, twin, 9, 9)
        arrive(2, piece)
        send(2, piece, y_down, 4, None, half, half, half_sem.at[1], 16)
        send(2, piece, twin, 10, 10)
        arrive(3, piece)
        send(3, piece, y_up, 5, 3)
        send(3, piece, y_down, 6, 4)
        send(3, piece, twin, 11, 11)

    def relay_far(piece):
        arrive(4, piece, 0, half)
        arrive(4, piece, half, half, 16)
        send(4, piece, x_flip, 7, 5)
        send(4, piece, twin, 12, 12)
        arrive(5, piece)
        send(5, piece, twin, 13, 13)
        arrive(6, piece)
        send(6, piece, twin, 14, 14)

    def finish(piece):
        arrive(7, piece)
        send(7, piece, twin, 15, 15)
        window = pl.ds(pl.multiple_of(piece * rows, 8), rows)

        for slot in range(16):
            if slot >= 8:
                arrive(slot, piece)
            to = pl.ds(slot * rows, rows)
            q_hi[to, :], q_lo[to, :] = split(held[slot, window, :])
        dims = (((1,), (1,)), ((), ()))
        product = functools.partial(lax.dot_general, dimension_numbers=dims, preferred_element_type=jnp.float32)
        scores[piece] = (
            product(q_hi[...], t_lo[...]) + product(q_lo[...], t_hi[...]) + product(q_hi[...], t_hi[...])
        )
        for slot in range(16):
            dx, dy = STEPS[slot % 8]
            owner = place(dx, -dy, slot // 8)
            block = scores.at[piece, pl.ds(slot * rows, rows), :]
            to = landed.at[layer, window, :]

            @pl.when(owner != layer)
            def _():
                pltpu.make_async_remote_copy(
                    src_ref=block, dst_ref=to, send_sem=out_sem.at[slot], recv_sem=in_sem.at[layer],
                    device_id={"layer": owner}, device_id_type=MESH,
                ).start()

            @pl.when(owner == layer)
            def _():
                landed[layer, window, :] = scores[piece, pl.ds(slot * rows, rows), :]

    @pl.loop(0, PIECES + 2)
    def _(step):
        @pl.when(step < PIECES)
        def _():
            relay_near(step)

        @pl.when((step >= 1) & (step < PIECES + 1))
        def _():
            relay_far(step - 1)

        @pl.when(step >= 2)
        def _():
            finish(step - 2)

    o_ref[...] = landed[layer]

    @pl.loop(1, layers)
    def _(step):
        peer = (layer + step) % layers
        block = landed.at[peer]
        pltpu.make_async_copy(block, block, in_sem.at[peer]).wait()
        o_ref[...] += landed[peer]

    for kind in range(16):
        if kind not in (6, 7):
            pltpu.make_async_copy(held.at[0], held.at[0], send_sem.at[kind]).wait()
    for kind in range(2):
        block = held.at[0, pl.ds(0, count // 2), :]
        pltpu.make_async_copy(block, block, half_sem.at[kind]).wait()
    for slot in range(16):
        dx, dy = STEPS[slot % 8]
        owner = place(dx, -dy, slot // 8)

        @pl.when(owner != layer)
        def _():
            pltpu.make_async_copy(landed.at[0], landed.at[0], out_sem.at[slot]).wait()


def transform(grads, eig_out, eig_in, damped_inverse):
    count, flat = grads.shape
    side_out, side_in = eig_out.shape[0], eig_in.shape[0]
    turn = functools.partial(jnp.einsum, precision=lax.Precision.HIGHEST)
    turned = turn("nrc,rs->nsc", grads.reshape(count, side_out, side_in), eig_out)
    turned = turn("nsc,ct->nst", turned, eig_in)
    turned = turned * damped_inverse.reshape(side_out, side_in)[None]
    turned = turn("nst,ct->nsc", turned, eig_in)
    turned = turn("nsc,rs->nrc", turned, eig_out)
    return turned.reshape(count, flat)


def shards(query_grads, train_grads, eig_out, eig_in, eig_values, train_ids):
    query, train = query_grads[0], train_grads[0]
    count, flat = query.shape
    t_count = train.shape[0]
    layers = lax.axis_size("layer")
    everyone = lax.axis_size("dp") * count
    damping = 0.1 * jnp.mean(eig_values[0])
    back = transform(query, eig_out[0], eig_in[0], 1.0 / (eig_values[0] + damping))
    rows = count // PIECES
    total = pl.pallas_call(
        kernel,
        out_shape=jax.ShapeDtypeStruct((count, t_count), jnp.float32),
        in_specs=[pl.BlockSpec(memory_space=pl.ANY)] * 2,
        out_specs=pl.BlockSpec(memory_space=pltpu.VMEM),
        scratch_shapes=[
            pltpu.VMEM((16, count, flat), jnp.float32),
            pltpu.VMEM((t_count, flat), jnp.float32),
            pltpu.VMEM((t_count, flat), jnp.bfloat16),
            pltpu.VMEM((t_count, flat), jnp.bfloat16),
            pltpu.VMEM((16 * rows, flat), jnp.bfloat16),
            pltpu.VMEM((16 * rows, flat), jnp.bfloat16),
            pltpu.VMEM((PIECES, 16 * rows, t_count), jnp.float32),
            pltpu.VMEM((layers, count, t_count), jnp.float32),
            pltpu.SemaphoreType.DMA,
            pltpu.SemaphoreType.DMA,
            pltpu.SemaphoreType.DMA((16,)),
            pltpu.SemaphoreType.DMA((2,)),
            pltpu.SemaphoreType.DMA((17, PIECES)),
            pltpu.SemaphoreType.DMA((16,)),
            pltpu.SemaphoreType.DMA((layers,)),
        ],
        compiler_params=pltpu.CompilerParams(
            collective_id=0, has_side_effects=True, vmem_limit_bytes=56 * 1024 * 1024
        ),
        cost_estimate=pl.CostEstimate(
            flops=6 * everyone * t_count * flat, bytes_accessed=4 * flat * (count + t_count), transcendentals=0
        ),
    )(back, train)
    position = train_ids.astype(jnp.float32) / float(CORPUS)
    rate = 0.1 + 0.45 * (1.0 + jnp.cos(jnp.pi * position))
    return total * rate[None, :] / math.sqrt(float(flat * layers))


def solution(mesh):
    placed = (
        P("layer", "dp", None),
        P("layer", "dp", None),
        P("layer", None, None),
        P("layer", None, None),
        P("layer", None),
        P("dp"),
    )
    return jax.shard_map(
        shards, mesh=mesh, in_specs=placed, out_specs=P("layer", "dp"), check_vma=False
    )
```

```python
import functools
import math

import jax
import jax.numpy as jnp
from jax import lax
from jax.experimental import pallas as pl
from jax.experimental.pallas import tpu as pltpu
from jax.sharding import PartitionSpec as P

CORPUS = 10000000
MESH = pl.DeviceIdType.MESH
ROWS = 8
GROUP = 16
PACK = 4

STEPS = ((0, 0), (0, 1), (0, -1), (1, 0), (0, 2), (1, 1), (1, -1), (1, 2))


def split(value):
    high = value.astype(jnp.bfloat16)
    low = (value - high.astype(jnp.float32)).astype(jnp.bfloat16)
    return high, low


def product(left, right, flipped=False):
    dims = (((1,), (1 if flipped else 0,)), ((), ()))
    dot = functools.partial(lax.dot_general, dimension_numbers=dims, preferred_element_type=jnp.float32)
    return dot(left[0], right[1]) + dot(left[1], right[0]) + dot(left[0], right[0])


def stack(flat):
    wide = PACK * 64
    return jnp.concatenate([flat[:, wide * i:wide * (i + 1)] for i in range(flat.shape[1] // wide)], axis=0)


def unstack(stacked):
    return jnp.concatenate([stacked[ROWS * i:ROWS * (i + 1), :] for i in range(stacked.shape[0] // ROWS)], axis=1)


def to_columns(stacked):
    turned = stacked.T
    side = turned.shape[0] // PACK
    return jnp.concatenate([turned[side * j:side * (j + 1), :] for j in range(PACK)], axis=1)


def from_columns(columns):
    wide = columns.shape[1] // PACK
    return jnp.concatenate([columns[:, wide * j:wide * (j + 1)] for j in range(PACK)], axis=0).T


def spread(basis, size, index, lane):
    side = basis.shape[0]
    iota = functools.partial(lax.broadcasted_iota, jnp.int32)
    tall = (index(iota((size, side), 0)) == iota((size, side), 1)).astype(jnp.bfloat16)
    wide = (iota((side, size), 0) == index(iota((side, size), 1))).astype(jnp.bfloat16)
    same = lane(iota((size, size), 0)) == lane(iota((size, size), 1))
    dot = functools.partial(jnp.dot, preferred_element_type=jnp.float32)
    return [
        jnp.where(same, dot(dot(tall, part).astype(jnp.bfloat16), wide), 0.0).astype(jnp.bfloat16)
        for part in split(basis)
    ]


def rotate(grads, out_op, in_op, inverse):
    parts = grads.shape[0] // ROWS
    tall = stack(grads[:ROWS]).shape[0]

    def each(turn, value, size):
        return jnp.concatenate([turn(value[size * k:size * (k + 1)]) for k in range(parts)], axis=0)

    value = each(stack, grads, ROWS)
    value = product(split(value), in_op)
    value = each(to_columns, value, tall)
    value = product(split(value), out_op)
    value = value * jnp.concatenate([inverse] * parts, axis=0)
    value = product(split(value), out_op, True)
    value = each(from_columns, value, 64)
    value = product(split(value), in_op, True)
    return each(unstack, value, tall)


def kernel(q_ref, t_ref, eig_out_ref, eig_in_ref, values_ref, o_ref,
           held, q_land, t_land, t_hi, t_lo, q_hi, q_lo, out_hi, out_lo, in_hi, in_lo, inverse,
           scores, landed, sums, crossed, load_sem, t_sem, send_sem, recv_sem, out_sem, in_sem, cross_sem):
    layer = lax.axis_index("layer")
    dp = lax.axis_index("dp")
    core, y, x = dp % 2, (dp // 2) % 4, dp // 8
    z, side = layer // 2, layer % 2
    count = q_ref.shape[0]
    pieces = count // ROWS
    depth = landed.shape[1]

    def place(dx, dy, dc):
        return (((x + dx) % 2) * 4 + (y + dy + 4) % 4) * 2 + (core + dc) % 2

    x_flip, y_up, y_down, twin = place(1, 0, 0), place(0, 1, 0), place(0, -1, 0), place(0, 0, 1)
    across = z * 2 + 1 - side

    load = pltpu.make_async_copy(q_ref, q_land, load_sem)
    load.start()
    t_load = pltpu.make_async_copy(t_ref, t_land, t_sem)
    t_load.start()

    barrier = pltpu.get_barrier_semaphore()
    for other in (x_flip, y_up, y_down, twin):
        pl.semaphore_signal(barrier, inc=1, device_id={"dp": other}, device_id_type=MESH)
    pl.semaphore_signal(barrier, inc=1, device_id={"layer": across}, device_id_type=MESH)

    @pl.loop(1, depth)
    def _(step):
        other = ((z + step) % depth) * 2 + side
        pl.semaphore_signal(barrier, inc=1, device_id={"layer": other}, device_id_type=MESH)

    def send(slot, piece, target, to_slot, kind):
        window = pl.ds(pl.multiple_of(piece * ROWS, ROWS), ROWS)
        pltpu.make_async_remote_copy(
            src_ref=held.at[slot, window, :],
            dst_ref=held.at[to_slot, window, :],
            send_sem=send_sem.at[kind],
            recv_sem=recv_sem.at[to_slot, piece],
            device_id={"dp": target},
            device_id_type=MESH,
        ).start()

    def to_twin(slot, piece):
        send(slot, piece, twin, 8 + slot, 9 + slot)

    def arrive(slot, piece):
        block = held.at[slot, pl.ds(pl.multiple_of(piece * ROWS, ROWS), ROWS), :]
        pltpu.make_async_copy(block, block, recv_sem.at[slot, piece]).wait()

    out_hi[...], out_lo[...] = spread(
        eig_out_ref[...], out_hi.shape[0], lambda a: (a % 128) // ROWS * PACK + a // 128, lambda a: a % ROWS
    )
    in_hi[...], in_lo[...] = spread(eig_in_ref[...], in_hi.shape[0], lambda a: a % 64, lambda a: a // 64)
    values = values_ref[...]
    damped = 1.0 / (values + 0.1 * jnp.mean(values))
    inverse[...] = to_columns(stack(jnp.broadcast_to(damped, (ROWS, damped.shape[1]))))

    load.wait()

    @pl.loop(0, count // GROUP)
    def _(group):
        window = pl.ds(pl.multiple_of(group * GROUP, GROUP), GROUP)
        held[0, window, :] = rotate(
            q_land[window, :], (out_hi[...], out_lo[...]), (in_hi[...], in_lo[...]), inverse[...]
        )

        @pl.when(group == 0)
        def _():
            pl.semaphore_wait(barrier, 5 + depth - 1)

        for k in range(GROUP // ROWS):
            piece = group * (GROUP // ROWS) + k
            send(0, piece, y_up, 1, 0)
            send(0, piece, y_down, 2, 1)
            send(0, piece, x_flip, 3, 2)
            to_twin(0, piece)

    t_load.wait()
    t_count = t_ref.shape[0]

    @pl.loop(0, t_ref.shape[1] // t_count)
    def _(tile):
        window = pl.ds(pl.multiple_of(tile * t_count, t_count), t_count)
        t_hi[window, :], t_lo[window, :] = split(t_land[:, window].T)

    def relay_near(piece):
        way = piece % 3
        arrive(1, piece)

        @pl.when(way != 1)
        def _():
            send(1, piece, y_up, 4, 3)

        @pl.when(way == 2)
        def _():
            send(1, piece, x_flip, 5, 5)

        to_twin(1, piece)
        arrive(2, piece)

        @pl.when(way == 1)
        def _():
            send(2, piece, y_down, 4, 4)

        to_twin(2, piece)
        arrive(3, piece)

        @pl.when(way != 2)
        def _():
            send(3, piece, y_up, 5, 6)

        send(3, piece, y_down, 6, 7)
        to_twin(3, piece)

    def relay_far(piece):
        arrive(4, piece)
        send(4, piece, x_flip, 7, 8)
        to_twin(4, piece)
        arrive(5, piece)
        to_twin(5, piece)
        arrive(6, piece)
        to_twin(6, piece)

    def score(piece):
        arrive(7, piece)
        to_twin(7, piece)
        window = pl.ds(pl.multiple_of(piece * ROWS, ROWS), ROWS)
        for slot in range(8, 16):
            arrive(slot, piece)
        for slot in range(8):
            to = pl.ds(slot * 2 * ROWS, 2 * ROWS)
            both = jnp.concatenate([held[slot, window, :], held[8 + slot, window, :]], axis=0)
            q_hi[to, :], q_lo[to, :] = split(both)
        scores[piece] = product((q_hi[...], q_lo[...]), (t_hi[...], t_lo[...]))
        for slot in range(8):
            dx, dy = STEPS[slot]
            owner = place(dx, -dy, 0) // 2
            block = scores.at[piece, pl.ds(slot * 2 * ROWS, 2 * ROWS), :]

            @pl.when(owner != z)
            def _():
                pltpu.make_async_remote_copy(
                    src_ref=block, dst_ref=landed.at[piece, z], send_sem=out_sem.at[slot], recv_sem=in_sem.at[piece],
                    device_id={"layer": owner * 2 + side}, device_id_type=MESH,
                ).start()

            @pl.when(owner == z)
            def _():
                landed[piece, z] = scores[piece, pl.ds(slot * 2 * ROWS, 2 * ROWS), :]

    kept = (core + side) % 2

    def gather_depth(piece):
        block = landed.at[piece, pl.ds(0, depth - 1)]
        pltpu.make_async_copy(block, block, in_sem.at[piece]).wait()
        sums[piece] = jnp.sum(landed[piece], axis=0)
        pltpu.make_async_remote_copy(
            src_ref=sums.at[piece, pl.ds(pl.multiple_of((1 - kept) * ROWS, ROWS), ROWS), :],
            dst_ref=crossed.at[piece],
            send_sem=cross_sem.at[0], recv_sem=cross_sem.at[1],
            device_id={"layer": across}, device_id_type=MESH,
        ).start()

    @pl.loop(0, pieces + 4)
    def _(step):
        @pl.when(step < pieces)
        def _():
            relay_near(step)

        @pl.when((step >= 2) & (step < pieces + 2))
        def _():
            relay_far(step - 2)

        @pl.when((step >= 3) & (step < pieces + 3))
        def _():
            score(step - 3)

        @pl.when(step >= 4)
        def _():
            gather_depth(step - 4)

    pltpu.make_async_copy(crossed, crossed, cross_sem.at[1]).wait()

    @pl.loop(0, pieces)
    def _(piece):
        window = pl.ds(pl.multiple_of(piece * ROWS, ROWS), ROWS)
        mine = pl.ds(pl.multiple_of(kept * ROWS, ROWS), ROWS)
        o_ref[window, :] = sums[piece, mine, :] + crossed[piece]

    pltpu.make_async_copy(crossed, crossed, cross_sem.at[0]).wait()
    by_way = [len([piece for piece in range(pieces) if piece % 3 == way]) for way in range(3)]
    sent = {3: by_way[0] + by_way[2], 4: by_way[1], 5: by_way[2], 6: by_way[0] + by_way[1]}
    for kind in range(17):
        block = held.at[0, pl.ds(0, sent.get(kind, pieces) * ROWS), :]
        pltpu.make_async_copy(block, block, send_sem.at[kind]).wait()
    for slot in range(8):
        dx, dy = STEPS[slot]
        owner = place(dx, -dy, 0) // 2

        @pl.when(owner != z)
        def _():
            block = landed.at[:, 0]
            pltpu.make_async_copy(block, block, out_sem.at[slot]).wait()


def shards(query_grads, train_grads, eig_out, eig_in, eig_values, train_ids):
    query, train = query_grads[0], train_grads[0]
    count, flat = query.shape
    t_count = train.shape[0]
    layers = lax.axis_size("layer")
    everyone = lax.axis_size("dp") * count
    pieces = count // ROWS
    side = eig_out.shape[1]
    f32, bf16 = jnp.float32, jnp.bfloat16
    vmem = pl.BlockSpec(memory_space=pltpu.VMEM)
    total = pl.pallas_call(
        kernel,
        out_shape=jax.ShapeDtypeStruct((count, t_count), f32),
        in_specs=[pl.BlockSpec(memory_space=pl.ANY)] * 2 + [vmem] * 3,
        out_specs=vmem,
        scratch_shapes=[
            pltpu.VMEM((16, count, flat), f32),
            pltpu.VMEM((count, flat), f32),
            pltpu.VMEM((t_count, flat), f32),
            pltpu.VMEM((flat, t_count), bf16),
            pltpu.VMEM((flat, t_count), bf16),
            pltpu.VMEM((16 * ROWS, flat), bf16),
            pltpu.VMEM((16 * ROWS, flat), bf16),
            pltpu.VMEM((side * ROWS, side * ROWS), bf16),
            pltpu.VMEM((side * ROWS, side * ROWS), bf16),
            pltpu.VMEM((side * PACK, side * PACK), bf16),
            pltpu.VMEM((side * PACK, side * PACK), bf16),
            pltpu.VMEM((side, side * ROWS), f32),
            pltpu.VMEM((pieces, 16 * ROWS, t_count), f32),
            pltpu.VMEM((pieces, layers // 2, 2 * ROWS, t_count), f32),
            pltpu.VMEM((pieces, 2 * ROWS, t_count), f32),
            pltpu.VMEM((pieces, ROWS, t_count), f32),
            pltpu.SemaphoreType.DMA,
            pltpu.SemaphoreType.DMA,
            pltpu.SemaphoreType.DMA((17,)),
            pltpu.SemaphoreType.DMA((16, pieces)),
            pltpu.SemaphoreType.DMA((8,)),
            pltpu.SemaphoreType.DMA((pieces,)),
            pltpu.SemaphoreType.DMA((2,)),
        ],
        compiler_params=pltpu.CompilerParams(
            collective_id=0, has_side_effects=True, vmem_limit_bytes=56 * 1024 * 1024
        ),
        cost_estimate=pl.CostEstimate(
            flops=6 * everyone * t_count * flat, bytes_accessed=4 * flat * (count + t_count), transcendentals=0
        ),
    )(query, train, eig_out[0], eig_in[0], eig_values)
    position = train_ids.astype(f32) / float(CORPUS)
    rate = 0.1 + 0.45 * (1.0 + jnp.cos(jnp.pi * position))
    return total * rate[None, :] / math.sqrt(float(flat * layers))


def solution(mesh):
    placed = (
        P("layer", "dp", None),
        P("layer", "dp", None),
        P("layer", None, None),
        P("layer", None, None),
        P("layer", None),
        P("dp"),
    )
    return jax.shard_map(
        shards, mesh=mesh, in_specs=placed, out_specs=P("layer", "dp"), check_vma=False
    )
```

```python
import functools
import math

import jax
import jax.numpy as jnp
from jax import lax
from jax.experimental import pallas as pl
from jax.experimental.pallas import tpu as pltpu
from jax.sharding import PartitionSpec as P

CORPUS = 10000000
MESH = pl.DeviceIdType.MESH
ROWS = 8
GROUP = 16
PACK = 4

STEPS = ((0, 0), (0, 1), (0, -1), (1, 0), (0, 2), (1, 1), (1, -1), (1, 2))


def split(value):
    high = value.astype(jnp.bfloat16)
    low = (value - high.astype(jnp.float32)).astype(jnp.bfloat16)
    return high, low


def product(left, right, flipped=False):
    dims = (((1,), (1 if flipped else 0,)), ((), ()))
    dot = functools.partial(lax.dot_general, dimension_numbers=dims, preferred_element_type=jnp.float32)
    return dot(left[0], right[1]) + dot(left[1], right[0]) + dot(left[0], right[0])


def stack(flat):
    wide = PACK * 64
    return jnp.concatenate([flat[:, wide * i:wide * (i + 1)] for i in range(flat.shape[1] // wide)], axis=0)


def unstack(stacked):
    return jnp.concatenate([stacked[ROWS * i:ROWS * (i + 1), :] for i in range(stacked.shape[0] // ROWS)], axis=1)


def to_columns(stacked):
    turned = stacked.T
    side = turned.shape[0] // PACK
    return jnp.concatenate([turned[side * j:side * (j + 1), :] for j in range(PACK)], axis=1)


def from_columns(columns):
    wide = columns.shape[1] // PACK
    return jnp.concatenate([columns[:, wide * j:wide * (j + 1)] for j in range(PACK)], axis=0).T


def spread(basis, size, index, lane):
    side = basis.shape[0]
    iota = functools.partial(lax.broadcasted_iota, jnp.int32)
    tall = (index(iota((size, side), 0)) == iota((size, side), 1)).astype(jnp.bfloat16)
    wide = (iota((side, size), 0) == index(iota((side, size), 1))).astype(jnp.bfloat16)
    same = lane(iota((size, size), 0)) == lane(iota((size, size), 1))
    dot = functools.partial(jnp.dot, preferred_element_type=jnp.float32)
    return [
        jnp.where(same, dot(dot(tall, part).astype(jnp.bfloat16), wide), 0.0).astype(jnp.bfloat16)
        for part in split(basis)
    ]


def rotate(grads, out_op, in_op, inverse):
    parts = grads.shape[0] // ROWS
    tall = stack(grads[:ROWS]).shape[0]

    def each(turn, value, size):
        return jnp.concatenate([turn(value[size * k:size * (k + 1)]) for k in range(parts)], axis=0)

    value = each(stack, grads, ROWS)
    value = product(split(value), in_op)
    value = each(to_columns, value, tall)
    value = product(split(value), out_op)
    value = value * jnp.concatenate([inverse] * parts, axis=0)
    value = product(split(value), out_op, True)
    value = each(from_columns, value, 64)
    value = product(split(value), in_op, True)
    return each(unstack, value, tall)


def kernel(q_ref, t_ref, eig_out_ref, eig_in_ref, values_ref, ids_ref, o_ref,
           held, q_land, weight, t_land, t_hi, t_lo, q_hi, q_lo, out_hi, out_lo, in_hi, in_lo, inverse,
           scores, landed, direct, sums, crossed, load_sem, t_sem, send_sem, recv_sem, out_sem, in_sem, cross_sem):
    layer = lax.axis_index("layer")
    dp = lax.axis_index("dp")
    core, y, x = dp % 2, (dp // 2) % 4, dp // 8
    z, side = layer // 2, layer % 2
    count = q_ref.shape[0]
    pieces = count // ROWS
    depth = landed.shape[1]
    last = pieces - 1
    layers = direct.shape[0]

    def place(dx, dy, dc):
        return (((x + dx) % 2) * 4 + (y + dy + 4) % 4) * 2 + (core + dc) % 2

    x_flip, y_up, y_down, twin = place(1, 0, 0), place(0, 1, 0), place(0, -1, 0), place(0, 0, 1)
    across = z * 2 + 1 - side

    load = pltpu.make_async_copy(q_ref, q_land, load_sem)
    load.start()
    t_load = pltpu.make_async_copy(t_ref, t_land, t_sem)

    barrier = pltpu.get_barrier_semaphore()
    for other in (x_flip, y_up, y_down, twin):
        pl.semaphore_signal(barrier, inc=1, device_id={"dp": other}, device_id_type=MESH)

    @pl.loop(1, layers)
    def _(step):
        pl.semaphore_signal(barrier, inc=1, device_id={"layer": (layer + step) % layers}, device_id_type=MESH)

    def send(slot, piece, target, to_slot, kind):
        window = pl.ds(pl.multiple_of(piece * ROWS, ROWS), ROWS)
        pltpu.make_async_remote_copy(
            src_ref=held.at[slot, window, :],
            dst_ref=held.at[to_slot, window, :],
            send_sem=send_sem.at[kind],
            recv_sem=recv_sem.at[to_slot, piece],
            device_id={"dp": target},
            device_id_type=MESH,
        ).start()

    def to_twin(slot, piece):
        send(slot, piece, twin, 8 + slot, 9 + slot)

    def arrive(slot, piece):
        block = held.at[slot, pl.ds(pl.multiple_of(piece * ROWS, ROWS), ROWS), :]
        pltpu.make_async_copy(block, block, recv_sem.at[slot, piece]).wait()

    out_hi[...], out_lo[...] = spread(
        eig_out_ref[...], out_hi.shape[0], lambda a: (a % 128) // ROWS * PACK + a // 128, lambda a: a % ROWS
    )
    in_hi[...], in_lo[...] = spread(eig_in_ref[...], in_hi.shape[0], lambda a: a % 64, lambda a: a // 64)
    values = values_ref[...]
    damped = 1.0 / (values + 0.1 * jnp.mean(values))
    inverse[...] = to_columns(stack(jnp.broadcast_to(damped, (ROWS, damped.shape[1]))))

    load.wait()
    t_load.start()

    @pl.loop(0, count // GROUP)
    def _(group):
        window = pl.ds(pl.multiple_of(group * GROUP, GROUP), GROUP)
        held[0, window, :] = rotate(
            q_land[window, :], (out_hi[...], out_lo[...]), (in_hi[...], in_lo[...]), inverse[...]
        )

        @pl.when(group == 0)
        def _():
            pl.semaphore_wait(barrier, 4 + layers - 1)

        for k in range(GROUP // ROWS):
            piece = group * (GROUP // ROWS) + k
            send(0, piece, y_up, 1, 0)
            send(0, piece, y_down, 2, 1)
            send(0, piece, x_flip, 3, 2)
            to_twin(0, piece)

    position = ids_ref[...].astype(jnp.float32) / float(CORPUS)
    rate = 0.1 + 0.45 * (1.0 + jnp.cos(jnp.pi * position))
    weight[...] = rate / math.sqrt(float(q_ref.shape[1] * landed.shape[1] * 2))

    t_load.wait()
    t_count = t_ref.shape[0]

    @pl.loop(0, t_ref.shape[1] // t_count)
    def _(tile):
        window = pl.ds(pl.multiple_of(tile * t_count, t_count), t_count)
        t_hi[window, :], t_lo[window, :] = split(t_land[:, window].T)

    def relay_rows(piece):
        way = piece % 3
        arrive(1, piece)

        @pl.when(way != 1)
        def _():
            send(1, piece, y_up, 4, 3)

        @pl.when(way == 2)
        def _():
            send(1, piece, x_flip, 5, 5)

        to_twin(1, piece)
        arrive(2, piece)

        @pl.when(way == 1)
        def _():
            send(2, piece, y_down, 4, 4)

        to_twin(2, piece)

    def relay_flip(piece):
        arrive(3, piece)

        @pl.when(piece % 3 != 2)
        def _():
            send(3, piece, y_up, 5, 6)

        send(3, piece, y_down, 6, 7)
        to_twin(3, piece)

    def relay_far(piece):
        arrive(4, piece)
        send(4, piece, x_flip, 7, 8)
        to_twin(4, piece)

    def share_last(piece):
        for slot in (7, 5, 6):
            arrive(slot, piece)
            to_twin(slot, piece)

    def score(piece, part):
        window = pl.ds(pl.multiple_of(piece * ROWS, ROWS), ROWS)
        slots = range(4 * part, 4 * part + 4)
        for slot in slots:
            arrive(8 + slot, piece)
        for at, slot in enumerate(slots):
            to = pl.ds(at * 2 * ROWS, 2 * ROWS)
            both = jnp.concatenate([held[slot, window, :], held[8 + slot, window, :]], axis=0)
            q_hi[to, :], q_lo[to, :] = split(both)
        scores[piece, part] = product((q_hi[...], q_lo[...]), (t_hi[...], t_lo[...]))
        for at, slot in enumerate(slots):
            dx, dy = STEPS[slot]
            owner = place(dx, -dy, 0) // 2

            @pl.when((piece < last) & (owner != z))
            def _():
                pltpu.make_async_remote_copy(
                    src_ref=scores.at[piece, part, pl.ds(at * 2 * ROWS, 2 * ROWS), :], dst_ref=landed.at[piece, z],
                    send_sem=out_sem.at[0], recv_sem=in_sem.at[piece],
                    device_id={"layer": owner * 2 + side}, device_id_type=MESH,
                ).start()

            @pl.when((piece < last) & (owner == z))
            def _():
                landed[piece, z] = scores[piece, part, pl.ds(at * 2 * ROWS, 2 * ROWS), :]

            for other in range(2):
                target = owner * 2 + (core + other) % 2
                block = pl.ds((at * 2 + other) * ROWS, ROWS)

                @pl.when((piece == last) & (target != layer))
                def _():
                    pltpu.make_async_remote_copy(
                        src_ref=scores.at[last, part, block, :], dst_ref=direct.at[layer],
                        send_sem=out_sem.at[1], recv_sem=in_sem.at[last],
                        device_id={"layer": target}, device_id_type=MESH,
                    ).start()

                @pl.when((piece == last) & (target == layer))
                def _():
                    direct[layer] = scores[last, part, block, :]

    kept = (core + side) % 2

    def gather_depth(piece):
        block = landed.at[piece, pl.ds(0, depth - 1)]
        pltpu.make_async_copy(block, block, in_sem.at[piece]).wait()
        sums[piece] = jnp.sum(landed[piece], axis=0)
        pltpu.make_async_remote_copy(
            src_ref=sums.at[piece, pl.ds(pl.multiple_of((1 - kept) * ROWS, ROWS), ROWS), :],
            dst_ref=crossed.at[piece],
            send_sem=cross_sem.at[0], recv_sem=cross_sem.at[1],
            device_id={"layer": across}, device_id_type=MESH,
        ).start()

    stages = (
        (0, relay_rows),
        (2, relay_flip),
        (3, lambda piece: score(piece, 0)),
        (5, relay_far),
        (8, share_last),
        (9, lambda piece: score(piece, 1)),
    )

    @pl.loop(0, pieces + stages[-1][0])
    def _(step):
        for behind, stage in stages:
            pl.when((step >= behind) & (step < pieces + behind))(functools.partial(stage, step - behind))

    by_way = [len([piece for piece in range(pieces) if piece % 3 == way]) for way in range(3)]
    sent = {3: by_way[0] + by_way[2], 4: by_way[1], 5: by_way[2], 6: by_way[0] + by_way[1]}
    for kind in range(17):
        block = held.at[0, pl.ds(0, sent.get(kind, pieces) * ROWS), :]
        pltpu.make_async_copy(block, block, send_sem.at[kind]).wait()

    pl.loop(0, last)(gather_depth)
    pltpu.make_async_copy(crossed, crossed, cross_sem.at[1]).wait()

    @pl.loop(0, last)
    def _(piece):
        window = pl.ds(pl.multiple_of(piece * ROWS, ROWS), ROWS)
        mine = pl.ds(pl.multiple_of(kept * ROWS, ROWS), ROWS)
        o_ref[window, :] = (sums[piece, mine, :] + crossed[piece]) * weight[...]

    pltpu.make_async_copy(crossed, crossed, cross_sem.at[0]).wait()
    block = landed.at[:, pl.ds(0, depth - 1)]
    pltpu.make_async_copy(block, block, out_sem.at[0]).wait()
    block = direct.at[pl.ds(0, direct.shape[0] - 1)]
    pltpu.make_async_copy(block, block, out_sem.at[1]).wait()
    pltpu.make_async_copy(block, block, in_sem.at[last]).wait()
    o_ref[pl.ds(last * ROWS, ROWS), :] = jnp.sum(direct[...], axis=0) * weight[...]


def shards(query_grads, train_grads, eig_out, eig_in, eig_values, train_ids):
    query, train = query_grads[0], train_grads[0]
    count, flat = query.shape
    t_count = train.shape[0]
    layers = lax.axis_size("layer")
    everyone = lax.axis_size("dp") * count
    pieces = count // ROWS
    side = eig_out.shape[1]
    f32, bf16 = jnp.float32, jnp.bfloat16
    vmem = pl.BlockSpec(memory_space=pltpu.VMEM)
    return pl.pallas_call(
        kernel,
        out_shape=jax.ShapeDtypeStruct((count, t_count), f32),
        in_specs=[pl.BlockSpec(memory_space=pl.ANY)] * 2 + [vmem] * 4,
        out_specs=vmem,
        scratch_shapes=[
            pltpu.VMEM((16, count, flat), f32),
            pltpu.VMEM((count, flat), f32),
            pltpu.VMEM((1, t_count), f32),
            pltpu.VMEM((t_count, flat), f32),
            pltpu.VMEM((flat, t_count), bf16),
            pltpu.VMEM((flat, t_count), bf16),
            pltpu.VMEM((8 * ROWS, flat), bf16),
            pltpu.VMEM((8 * ROWS, flat), bf16),
            pltpu.VMEM((side * ROWS, side * ROWS), bf16),
            pltpu.VMEM((side * ROWS, side * ROWS), bf16),
            pltpu.VMEM((side * PACK, side * PACK), bf16),
            pltpu.VMEM((side * PACK, side * PACK), bf16),
            pltpu.VMEM((side, side * ROWS), f32),
            pltpu.VMEM((pieces, 2, 8 * ROWS, t_count), f32),
            pltpu.VMEM((pieces - 1, layers // 2, 2 * ROWS, t_count), f32),
            pltpu.VMEM((layers, ROWS, t_count), f32),
            pltpu.VMEM((pieces - 1, 2 * ROWS, t_count), f32),
            pltpu.VMEM((pieces - 1, ROWS, t_count), f32),
            pltpu.SemaphoreType.DMA,
            pltpu.SemaphoreType.DMA,
            pltpu.SemaphoreType.DMA((17,)),
            pltpu.SemaphoreType.DMA((16, pieces)),
            pltpu.SemaphoreType.DMA((2,)),
            pltpu.SemaphoreType.DMA((pieces,)),
            pltpu.SemaphoreType.DMA((2,)),
        ],
        compiler_params=pltpu.CompilerParams(
            collective_id=0, has_side_effects=True, vmem_limit_bytes=56 * 1024 * 1024
        ),
        cost_estimate=pl.CostEstimate(
            flops=6 * everyone * t_count * flat, bytes_accessed=4 * flat * (count + t_count), transcendentals=0
        ),
    )(query, train, eig_out[0], eig_in[0], eig_values, train_ids[None])


def solution(mesh):
    placed = (
        P("layer", "dp", None),
        P("layer", "dp", None),
        P("layer", None, None),
        P("layer", None, None),
        P("layer", None),
        P("dp"),
    )
    return jax.shard_map(
        shards, mesh=mesh, in_specs=placed, out_specs=P("layer", "dp"), check_vma=False
    )
```

```python
import functools
import math
import operator

import jax
import jax.numpy as jnp
from jax import lax
from jax.experimental import pallas as pl
from jax.experimental.pallas import tpu as pltpu
from jax.sharding import PartitionSpec as P

CORPUS = 10000000
MESH = pl.DeviceIdType.MESH
ROWS = 8
GROUP = 16
WAYS = (0, 1, 2, 1, 0, 2, 1, 0)
PACK = 4

STEPS = ((0, 0), (0, 1), (0, -1), (1, 0), (0, 2), (1, 1), (1, -1), (1, 2))


def split(value):
    high = value.astype(jnp.bfloat16)
    low = (value - high.astype(jnp.float32)).astype(jnp.bfloat16)
    return high, low


def product(left, right, flipped=False):
    dims = (((1,), (1 if flipped else 0,)), ((), ()))
    dot = functools.partial(lax.dot_general, dimension_numbers=dims, preferred_element_type=jnp.float32)
    return dot(left[0], right[1]) + dot(left[1], right[0]) + dot(left[0], right[0])


def stack(flat):
    wide = PACK * 64
    return jnp.concatenate([flat[:, wide * i:wide * (i + 1)] for i in range(flat.shape[1] // wide)], axis=0)


def unstack(stacked):
    return jnp.concatenate([stacked[ROWS * i:ROWS * (i + 1), :] for i in range(stacked.shape[0] // ROWS)], axis=1)


def to_columns(stacked):
    turned = stacked.T
    side = turned.shape[0] // PACK
    return jnp.concatenate([turned[side * j:side * (j + 1), :] for j in range(PACK)], axis=1)


def from_columns(columns):
    wide = columns.shape[1] // PACK
    return jnp.concatenate([columns[:, wide * j:wide * (j + 1)] for j in range(PACK)], axis=0).T


def spread(basis, size, index, lane):
    side = basis.shape[0]
    iota = functools.partial(lax.broadcasted_iota, jnp.int32)
    tall = (index(iota((size, side), 0)) == iota((size, side), 1)).astype(jnp.bfloat16)
    wide = (iota((side, size), 0) == index(iota((side, size), 1))).astype(jnp.bfloat16)
    same = lane(iota((size, size), 0)) == lane(iota((size, size), 1))
    dot = functools.partial(jnp.dot, preferred_element_type=jnp.float32)
    return [
        jnp.where(same, dot(dot(tall, part).astype(jnp.bfloat16), wide), 0.0).astype(jnp.bfloat16)
        for part in split(basis)
    ]


def rotate(grads, out_op, in_op, inverse):
    parts = grads.shape[0] // ROWS
    tall = stack(grads[:ROWS]).shape[0]

    def each(turn, value, size):
        return jnp.concatenate([turn(value[size * k:size * (k + 1)]) for k in range(parts)], axis=0)

    value = each(stack, grads, ROWS)
    value = product(split(value), in_op)
    value = each(to_columns, value, tall)
    value = product(split(value), out_op)
    value = value * jnp.concatenate([inverse] * parts, axis=0)
    value = product(split(value), out_op, True)
    value = each(from_columns, value, 64)
    value = product(split(value), in_op, True)
    return each(unstack, value, tall)


def kernel(q_ref, t_ref, eig_out_ref, eig_in_ref, values_ref, ids_ref, o_ref,
           held, q_land, weight, t_land, t_hi, t_lo, q_hi, q_lo, out_hi, out_lo, in_hi, in_lo, inverse,
           scores, landed, direct, sums, crossed, load_sem, t_sem, send_sem, recv_sem, out_sem, in_sem, cross_sem):
    layer = lax.axis_index("layer")
    dp = lax.axis_index("dp")
    core, y, x = dp % 2, (dp // 2) % 4, dp // 8
    z, side = layer // 2, layer % 2
    count = q_ref.shape[0]
    pieces = count // ROWS
    depth = landed.shape[1]
    last = pieces - 1
    layers = direct.shape[0]

    def place(dx, dy, dc):
        return (((x + dx) % 2) * 4 + (y + dy + 4) % 4) * 2 + (core + dc) % 2

    x_flip, y_up, y_down, twin = place(1, 0, 0), place(0, 1, 0), place(0, -1, 0), place(0, 0, 1)
    across = z * 2 + 1 - side

    load = pltpu.make_async_copy(q_ref, q_land, load_sem)
    load.start()
    t_load = pltpu.make_async_copy(t_ref, t_land, t_sem)

    barrier = pltpu.get_barrier_semaphore()
    for other in (x_flip, y_up, y_down, twin):
        pl.semaphore_signal(barrier, inc=1, device_id={"dp": other}, device_id_type=MESH)

    @pl.loop(1, layers)
    def _(step):
        pl.semaphore_signal(barrier, inc=1, device_id={"layer": (layer + step) % layers}, device_id_type=MESH)

    def send(slot, piece, target, to_slot, kind):
        window = pl.ds(pl.multiple_of(piece * ROWS, ROWS), ROWS)
        pltpu.make_async_remote_copy(
            src_ref=held.at[slot, window, :],
            dst_ref=held.at[to_slot, window, :],
            send_sem=send_sem.at[kind],
            recv_sem=recv_sem.at[to_slot, piece],
            device_id={"dp": target},
            device_id_type=MESH,
        ).start()

    def to_twin(slot, piece, slots=1):
        window = pl.ds(pl.multiple_of(piece * ROWS, ROWS), ROWS)
        pltpu.make_async_remote_copy(
            src_ref=held.at[pl.ds(slot, slots), window, :],
            dst_ref=held.at[pl.ds(8 + slot, slots), window, :],
            send_sem=send_sem.at[9 + slot],
            recv_sem=recv_sem.at[8 + slot, piece],
            device_id={"dp": twin},
            device_id_type=MESH,
        ).start()

    def arrive(slot, piece, slots=1):
        block = held.at[pl.ds(slot, slots), pl.ds(pl.multiple_of(piece * ROWS, ROWS), ROWS), :]
        pltpu.make_async_copy(block, block, recv_sem.at[slot, piece]).wait()

    out_hi[...], out_lo[...] = spread(
        eig_out_ref[...], out_hi.shape[0], lambda a: (a % 128) // ROWS * PACK + a // 128, lambda a: a % ROWS
    )
    in_hi[...], in_lo[...] = spread(eig_in_ref[...], in_hi.shape[0], lambda a: a % 64, lambda a: a // 64)
    values = values_ref[...]
    damped = 1.0 / (values + 0.1 * jnp.mean(values))
    inverse[...] = to_columns(stack(jnp.broadcast_to(damped, (ROWS, damped.shape[1]))))

    load.wait()
    t_load.start()

    @pl.loop(0, count // GROUP)
    def _(group):
        window = pl.ds(pl.multiple_of(group * GROUP, GROUP), GROUP)
        held[0, window, :] = rotate(
            q_land[window, :], (out_hi[...], out_lo[...]), (in_hi[...], in_lo[...]), inverse[...]
        )

        @pl.when(group == 0)
        def _():
            pl.semaphore_wait(barrier, 4 + layers - 1)

        for k in range(GROUP // ROWS):
            piece = group * (GROUP // ROWS) + k
            send(0, piece, y_up, 1, 0)
            send(0, piece, y_down, 2, 1)
            send(0, piece, x_flip, 3, 2)
            to_twin(0, piece)

    position = ids_ref[...].astype(jnp.float32) / float(CORPUS)
    rate = 0.1 + 0.45 * (1.0 + jnp.cos(jnp.pi * position))
    weight[...] = rate / math.sqrt(float(q_ref.shape[1] * landed.shape[1] * 2))

    t_load.wait()
    t_count = t_ref.shape[0]

    @pl.loop(0, t_ref.shape[1] // t_count)
    def _(tile):
        window = pl.ds(pl.multiple_of(tile * t_count, t_count), t_count)
        t_hi[window, :], t_lo[window, :] = split(t_land[:, window].T)

    def goes(piece, way):
        return functools.reduce(operator.or_, [piece == at for at in range(pieces) if WAYS[at] == way])

    def relay_rows(piece):
        arrive(1, piece)

        @pl.when(jnp.logical_not(goes(piece, 1)))
        def _():
            send(1, piece, y_up, 4, 3)

        @pl.when(goes(piece, 2))
        def _():
            send(1, piece, x_flip, 5, 5)

        arrive(2, piece)

        @pl.when(goes(piece, 1))
        def _():
            send(2, piece, y_down, 4, 4)

        to_twin(1, piece, 2)

    def relay_flip(piece):
        arrive(3, piece)

        @pl.when(jnp.logical_not(goes(piece, 2)))
        def _():
            send(3, piece, y_up, 5, 6)

        send(3, piece, y_down, 6, 7)
        to_twin(3, piece)

    def relay_far(piece):
        arrive(4, piece)
        send(4, piece, x_flip, 7, 8)
        to_twin(4, piece)

    def share_last(piece):
        arrive(7, piece)
        to_twin(7, piece)
        arrive(5, piece)
        arrive(6, piece)
        to_twin(5, piece, 2)

    def take(piece, part):
        window = pl.ds(pl.multiple_of(piece * ROWS, ROWS), ROWS)
        for slot, slots in ((8 + 4 * part, 1), (9 + 4 * part, 2), (11 + 4 * part, 1)):
            arrive(slot, piece, slots)
        for at in range(4):
            slot = 4 * part + at
            to = pl.ds(slot * 2 * ROWS, 2 * ROWS)
            both = jnp.concatenate([held[slot, window, :], held[8 + slot, window, :]], axis=0)
            q_hi[to, :], q_lo[to, :] = split(both)

    def give(piece, part, both):
        scores[piece, part] = both[part * 8 * ROWS:(part + 1) * 8 * ROWS]
        slots = range(4 * part, 4 * part + 4)
        for at, slot in enumerate(slots):
            dx, dy = STEPS[slot]
            owner = place(dx, -dy, 0) // 2

            @pl.when((piece < last) & (owner != z))
            def _():
                pltpu.make_async_remote_copy(
                    src_ref=scores.at[piece, part, pl.ds(at * 2 * ROWS, 2 * ROWS), :], dst_ref=landed.at[piece, z],
                    send_sem=out_sem.at[0], recv_sem=in_sem.at[piece],
                    device_id={"layer": owner * 2 + side}, device_id_type=MESH,
                ).start()

            @pl.when((piece < last) & (owner == z))
            def _():
                landed[piece, z] = scores[piece, part, pl.ds(at * 2 * ROWS, 2 * ROWS), :]

            for other in range(2):
                target = owner * 2 + (core + other) % 2
                block = pl.ds((at * 2 + other) * ROWS, ROWS)

                @pl.when((piece == last) & (target != layer))
                def _():
                    pltpu.make_async_remote_copy(
                        src_ref=scores.at[last, part, block, :], dst_ref=direct.at[layer],
                        send_sem=out_sem.at[1], recv_sem=in_sem.at[last],
                        device_id={"layer": target}, device_id_type=MESH,
                    ).start()

                @pl.when((piece == last) & (target == layer))
                def _():
                    direct[layer] = scores[last, part, block, :]

    kept = (core + side) % 2

    def gather_depth(piece):
        block = landed.at[piece, pl.ds(0, depth - 1)]
        pltpu.make_async_copy(block, block, in_sem.at[piece]).wait()
        sums[piece] = jnp.sum(landed[piece], axis=0)
        pltpu.make_async_remote_copy(
            src_ref=sums.at[piece, pl.ds(pl.multiple_of((1 - kept) * ROWS, ROWS), ROWS), :],
            dst_ref=crossed.at[piece],
            send_sem=cross_sem.at[0], recv_sem=cross_sem.at[1],
            device_id={"layer": across}, device_id_type=MESH,
        ).start()

    stages = ((0, relay_rows), (1, relay_flip), (5, relay_far), (6, share_last))
    score_behind = (6, 7)

    @pl.loop(0, pieces + score_behind[1])
    def _(step):
        for behind, stage in stages:
            pl.when((step >= behind) & (step < pieces + behind))(functools.partial(stage, step - behind))

        @pl.when(step >= score_behind[0])
        def _():
            valid = [(step >= behind) & (step < pieces + behind) for behind in score_behind]
            for part in range(2):
                pl.when(valid[part])(functools.partial(take, step - score_behind[part], part))
            both = product((q_hi[...], q_lo[...]), (t_hi[...], t_lo[...]))
            for part in (1, 0):
                pl.when(valid[part])(functools.partial(give, step - score_behind[part], part, both))

    by_way = [WAYS.count(way) for way in range(3)]
    sent = {3: by_way[0] + by_way[2], 4: by_way[1], 5: by_way[2], 6: by_way[0] + by_way[1]}
    for kind in [kind for kind in range(17) if kind not in (11, 15)]:
        block = held.at[pl.ds(0, 2 if kind in (10, 14) else 1), pl.ds(0, sent.get(kind, pieces) * ROWS), :]
        pltpu.make_async_copy(block, block, send_sem.at[kind]).wait()

    pl.loop(0, last)(gather_depth)
    pltpu.make_async_copy(crossed, crossed, cross_sem.at[1]).wait()

    @pl.loop(0, last)
    def _(piece):
        window = pl.ds(pl.multiple_of(piece * ROWS, ROWS), ROWS)
        mine = pl.ds(pl.multiple_of(kept * ROWS, ROWS), ROWS)
        o_ref[window, :] = (sums[piece, mine, :] + crossed[piece]) * weight[...]

    pltpu.make_async_copy(crossed, crossed, cross_sem.at[0]).wait()
    block = landed.at[:, pl.ds(0, depth - 1)]
    pltpu.make_async_copy(block, block, out_sem.at[0]).wait()
    block = direct.at[pl.ds(0, direct.shape[0] - 1)]
    pltpu.make_async_copy(block, block, out_sem.at[1]).wait()
    pltpu.make_async_copy(block, block, in_sem.at[last]).wait()
    o_ref[pl.ds(last * ROWS, ROWS), :] = jnp.sum(direct[...], axis=0) * weight[...]


def shards(query_grads, train_grads, eig_out, eig_in, eig_values, train_ids):
    query, train = query_grads[0], train_grads[0]
    count, flat = query.shape
    t_count = train.shape[0]
    layers = lax.axis_size("layer")
    everyone = lax.axis_size("dp") * count
    pieces = count // ROWS
    side = eig_out.shape[1]
    f32, bf16 = jnp.float32, jnp.bfloat16
    vmem = pl.BlockSpec(memory_space=pltpu.VMEM)
    return pl.pallas_call(
        kernel,
        out_shape=jax.ShapeDtypeStruct((count, t_count), f32),
        in_specs=[pl.BlockSpec(memory_space=pl.ANY)] * 2 + [vmem] * 4,
        out_specs=vmem,
        scratch_shapes=[
            pltpu.VMEM((16, count, flat), f32),
            pltpu.VMEM((count, flat), f32),
            pltpu.VMEM((1, t_count), f32),
            pltpu.VMEM((t_count, flat), f32),
            pltpu.VMEM((flat, t_count), bf16),
            pltpu.VMEM((flat, t_count), bf16),
            pltpu.VMEM((16 * ROWS, flat), bf16),
            pltpu.VMEM((16 * ROWS, flat), bf16),
            pltpu.VMEM((side * ROWS, side * ROWS), bf16),
            pltpu.VMEM((side * ROWS, side * ROWS), bf16),
            pltpu.VMEM((side * PACK, side * PACK), bf16),
            pltpu.VMEM((side * PACK, side * PACK), bf16),
            pltpu.VMEM((side, side * ROWS), f32),
            pltpu.VMEM((pieces, 2, 8 * ROWS, t_count), f32),
            pltpu.VMEM((pieces - 1, layers // 2, 2 * ROWS, t_count), f32),
            pltpu.VMEM((layers, ROWS, t_count), f32),
            pltpu.VMEM((pieces - 1, 2 * ROWS, t_count), f32),
            pltpu.VMEM((pieces - 1, ROWS, t_count), f32),
            pltpu.SemaphoreType.DMA,
            pltpu.SemaphoreType.DMA,
            pltpu.SemaphoreType.DMA((17,)),
            pltpu.SemaphoreType.DMA((16, pieces)),
            pltpu.SemaphoreType.DMA((2,)),
            pltpu.SemaphoreType.DMA((pieces,)),
            pltpu.SemaphoreType.DMA((2,)),
        ],
        compiler_params=pltpu.CompilerParams(
            collective_id=0, has_side_effects=True, vmem_limit_bytes=56 * 1024 * 1024
        ),
        cost_estimate=pl.CostEstimate(
            flops=6 * everyone * t_count * flat, bytes_accessed=4 * flat * (count + t_count), transcendentals=0
        ),
    )(query, train, eig_out[0], eig_in[0], eig_values, train_ids[None])


def solution(mesh):
    placed = (
        P("layer", "dp", None),
        P("layer", "dp", None),
        P("layer", None, None),
        P("layer", None, None),
        P("layer", None),
        P("dp"),
    )
    return jax.shard_map(
        shards, mesh=mesh, in_specs=placed, out_specs=P("layer", "dp"), check_vma=False
    )
```

```python
import functools
import math
import operator

import jax
import jax.numpy as jnp
from jax import lax
from jax.experimental import pallas as pl
from jax.experimental.pallas import tpu as pltpu
from jax.sharding import PartitionSpec as P

CORPUS = 10000000
MESH = pl.DeviceIdType.MESH
ROWS = 8
GROUP = 16
WAYS = (0, 1, 2, 1, 0, 2, 1, 0)
PACK = 4

STEPS = ((0, 0), (0, 1), (0, -1), (1, 0), (0, 2), (1, 1), (1, -1), (1, 2))


def split(value):
    high = value.astype(jnp.bfloat16)
    low = (value - high.astype(jnp.float32)).astype(jnp.bfloat16)
    return high, low


def product(left, right, flipped=False):
    dims = (((1,), (1 if flipped else 0,)), ((), ()))
    dot = functools.partial(lax.dot_general, dimension_numbers=dims, preferred_element_type=jnp.float32)
    return dot(left[0], right[1]) + dot(left[1], right[0]) + dot(left[0], right[0])


def stack(flat):
    wide = PACK * 64
    return jnp.concatenate([flat[:, wide * i:wide * (i + 1)] for i in range(flat.shape[1] // wide)], axis=0)


def unstack(stacked):
    return jnp.concatenate([stacked[ROWS * i:ROWS * (i + 1), :] for i in range(stacked.shape[0] // ROWS)], axis=1)


def to_columns(stacked):
    turned = stacked.T
    side = turned.shape[0] // PACK
    return jnp.concatenate([turned[side * j:side * (j + 1), :] for j in range(PACK)], axis=1)


def from_columns(columns):
    wide = columns.shape[1] // PACK
    return jnp.concatenate([columns[:, wide * j:wide * (j + 1)] for j in range(PACK)], axis=0).T


def spread(basis, size, index, lane):
    side = basis.shape[0]
    iota = functools.partial(lax.broadcasted_iota, jnp.int32)
    tall = (index(iota((size, side), 0)) == iota((size, side), 1)).astype(jnp.bfloat16)
    wide = (iota((side, size), 0) == index(iota((side, size), 1))).astype(jnp.bfloat16)
    same = lane(iota((size, size), 0)) == lane(iota((size, size), 1))
    dot = functools.partial(jnp.dot, preferred_element_type=jnp.float32)
    return [
        jnp.where(same, dot(dot(tall, part).astype(jnp.bfloat16), wide), 0.0).astype(jnp.bfloat16)
        for part in split(basis)
    ]


def rotate(grads, out_op, in_op, inverse):
    parts = grads.shape[0] // ROWS
    tall = stack(grads[:ROWS]).shape[0]

    def each(turn, value, size):
        return jnp.concatenate([turn(value[size * k:size * (k + 1)]) for k in range(parts)], axis=0)

    value = each(stack, grads, ROWS)
    value = product(split(value), in_op)
    value = each(to_columns, value, tall)
    value = product(split(value), out_op)
    value = value * jnp.concatenate([inverse] * parts, axis=0)
    value = product(split(value), out_op, True)
    value = each(from_columns, value, 64)
    value = product(split(value), in_op, True)
    return each(unstack, value, tall)


def kernel(q_ref, t_ref, eig_out_hbm, eig_in_hbm, values_hbm, ids_hbm, o_ref,
           eig_out_ref, eig_in_ref, values_ref, ids_ref, small_sem,
           held, q_land, weight, t_land, t_hi, t_lo, q_hi, q_lo, out_hi, out_lo, in_hi, in_lo, inverse,
           scores, landed, direct, sums, crossed, load_sem, t_sem, send_sem, recv_sem, out_sem, in_sem, cross_sem):
    layer = lax.axis_index("layer")
    dp = lax.axis_index("dp")
    core, y, x = dp % 2, (dp // 2) % 4, dp // 8
    z, side = layer // 2, layer % 2
    count = q_ref.shape[0]
    pieces = count // ROWS
    depth = landed.shape[1]
    last = pieces - 1
    layers = direct.shape[0]

    def place(dx, dy, dc):
        return (((x + dx) % 2) * 4 + (y + dy + 4) % 4) * 2 + (core + dc) % 2

    x_flip, y_up, y_down, twin = place(1, 0, 0), place(0, 1, 0), place(0, -1, 0), place(0, 0, 1)
    across = z * 2 + 1 - side

    barrier = pltpu.get_barrier_semaphore()
    for other in (x_flip, y_up, y_down, twin):
        pl.semaphore_signal(barrier, inc=1, device_id={"dp": other}, device_id_type=MESH)

    @pl.loop(1, layers)
    def _(step):
        pl.semaphore_signal(barrier, inc=1, device_id={"layer": (layer + step) % layers}, device_id_type=MESH)

    small = [
        pltpu.make_async_copy(source, target, small_sem.at[at])
        for at, (source, target) in enumerate((
            (eig_out_hbm, eig_out_ref), (eig_in_hbm, eig_in_ref), (values_hbm, values_ref), (ids_hbm, ids_ref)
        ))
    ]
    for copy in small:
        copy.start()
    load = pltpu.make_async_copy(q_ref, q_land, load_sem)
    load.start()
    t_load = pltpu.make_async_copy(t_ref, t_land, t_sem)

    def send(slot, piece, target, to_slot, kind):
        window = pl.ds(pl.multiple_of(piece * ROWS, ROWS), ROWS)
        pltpu.make_async_remote_copy(
            src_ref=held.at[slot, window, :],
            dst_ref=held.at[to_slot, window, :],
            send_sem=send_sem.at[kind],
            recv_sem=recv_sem.at[to_slot, piece],
            device_id={"dp": target},
            device_id_type=MESH,
        ).start()

    def to_twin(slot, piece, slots=1, span=1):
        window = pl.ds(pl.multiple_of(piece * ROWS, ROWS), span * ROWS)
        pltpu.make_async_remote_copy(
            src_ref=held.at[pl.ds(slot, slots), window, :],
            dst_ref=held.at[pl.ds(8 + slot, slots), window, :],
            send_sem=send_sem.at[9 + slot],
            recv_sem=recv_sem.at[8 + slot, piece],
            device_id={"dp": twin},
            device_id_type=MESH,
        ).start()

    def arrive(slot, piece, slots=1, span=1):
        block = held.at[pl.ds(slot, slots), pl.ds(pl.multiple_of(piece * ROWS, ROWS), span * ROWS), :]
        pltpu.make_async_copy(block, block, recv_sem.at[slot, piece]).wait()

    for copy in small:
        copy.wait()
    out_hi[...], out_lo[...] = spread(
        eig_out_ref[...], out_hi.shape[0], lambda a: (a % 128) // ROWS * PACK + a // 128, lambda a: a % ROWS
    )
    in_hi[...], in_lo[...] = spread(eig_in_ref[...], in_hi.shape[0], lambda a: a % 64, lambda a: a // 64)
    values = values_ref[...]
    damped = 1.0 / (values + 0.1 * jnp.mean(values))
    inverse[...] = to_columns(stack(jnp.broadcast_to(damped, (ROWS, damped.shape[1]))))

    load.wait()
    t_load.start()

    def own(group):
        window = pl.ds(pl.multiple_of(group * GROUP, GROUP), GROUP)
        held[0, window, :] = rotate(
            q_land[window, :], (out_hi[...], out_lo[...]), (in_hi[...], in_lo[...]), inverse[...]
        )

        @pl.when(group == 0)
        def _():
            pl.semaphore_wait(barrier, 4 + layers - 1)

        for k in range(GROUP // ROWS):
            piece = group * (GROUP // ROWS) + k
            send(0, piece, y_up, 1, 0)
            send(0, piece, y_down, 2, 1)
            send(0, piece, x_flip, 3, 2)

        to_twin(0, group * (GROUP // ROWS), 1, GROUP // ROWS)

    pl.loop(0, 3)(own)

    position = ids_ref[...].astype(jnp.float32) / float(CORPUS)
    rate = 0.1 + 0.45 * (1.0 + jnp.cos(jnp.pi * position))
    weight[...] = rate / math.sqrt(float(q_ref.shape[1] * landed.shape[1] * 2))

    t_load.wait()
    t_count = t_ref.shape[0]

    @pl.loop(0, t_ref.shape[1] // t_count)
    def _(tile):
        window = pl.ds(pl.multiple_of(tile * t_count, t_count), t_count)
        t_hi[window, :], t_lo[window, :] = split(t_land[:, window].T)

    def goes(piece, way):
        return functools.reduce(operator.or_, [piece == at for at in range(pieces) if WAYS[at] == way])

    def relay_rows(piece):
        arrive(1, piece)

        @pl.when(jnp.logical_not(goes(piece, 1)))
        def _():
            send(1, piece, y_up, 4, 3)

        @pl.when(goes(piece, 2))
        def _():
            send(1, piece, x_flip, 5, 5)

        arrive(2, piece)

        @pl.when(goes(piece, 1))
        def _():
            send(2, piece, y_down, 4, 4)


    def relay_flip(piece):
        arrive(3, piece)

        @pl.when(jnp.logical_not(goes(piece, 2)))
        def _():
            send(3, piece, y_up, 5, 6)

        send(3, piece, y_down, 6, 7)

        @pl.when(piece % 2 == 1)
        def _():
            to_twin(1, piece - 1, 3, 2)

    def relay_far(piece):
        arrive(4, piece)
        send(4, piece, x_flip, 7, 8)
        to_twin(4, piece)

    def share_last(piece):
        arrive(7, piece)
        arrive(5, piece)
        arrive(6, piece)
        to_twin(5, piece, 3)

    def take(piece, part):
        window = pl.ds(pl.multiple_of(piece * ROWS, ROWS), ROWS)
        if part == 0:
            @pl.when(piece % 2 == 0)
            def _():
                arrive(8, piece, 1, 2)
                arrive(9, piece, 3, 2)
        else:
            arrive(12, piece)
            arrive(13, piece, 3)
        for at in range(4):
            slot = 4 * part + at
            to = pl.ds(slot * 2 * ROWS, 2 * ROWS)
            both = jnp.concatenate([held[slot, window, :], held[8 + slot, window, :]], axis=0)
            q_hi[to, :], q_lo[to, :] = split(both)

    def give(piece, part, both):
        scores[piece, part] = both[part * 8 * ROWS:(part + 1) * 8 * ROWS]
        slots = range(4 * part, 4 * part + 4)
        owners = [place(STEPS[slot][0], -STEPS[slot][1], 0) // 2 for slot in slots]

        @pl.when(piece < last)
        def _():
            for at, owner in enumerate(owners):
                block = pl.ds(at * 2 * ROWS, 2 * ROWS)

                @pl.when(owner != z)
                def _():
                    pltpu.make_async_remote_copy(
                        src_ref=scores.at[piece, part, block, :], dst_ref=landed.at[piece, z],
                        send_sem=out_sem.at[0], recv_sem=in_sem.at[piece],
                        device_id={"layer": owner * 2 + side}, device_id_type=MESH,
                    ).start()

                @pl.when(owner == z)
                def _():
                    landed[piece, z] = scores[piece, part, block, :]

        @pl.when(piece == last)
        def _():
            for at, owner in enumerate(owners):
                for other in range(2):
                    target = owner * 2 + (core + other) % 2
                    block = pl.ds((at * 2 + other) * ROWS, ROWS)

                    @pl.when(target != layer)
                    def _():
                        pltpu.make_async_remote_copy(
                            src_ref=scores.at[last, part, block, :], dst_ref=direct.at[layer],
                            send_sem=out_sem.at[1], recv_sem=in_sem.at[last],
                            device_id={"layer": target}, device_id_type=MESH,
                        ).start()

                    @pl.when(target == layer)
                    def _():
                        direct[layer] = scores[last, part, block, :]

    kept = (core + side) % 2

    def gather_depth(piece):
        block = landed.at[piece, pl.ds(0, depth - 1)]
        pltpu.make_async_copy(block, block, in_sem.at[piece]).wait()
        sums[piece] = jnp.sum(landed[piece], axis=0)
        pltpu.make_async_remote_copy(
            src_ref=sums.at[piece, pl.ds(pl.multiple_of((1 - kept) * ROWS, ROWS), ROWS), :],
            dst_ref=crossed.at[piece],
            send_sem=cross_sem.at[0], recv_sem=cross_sem.at[1],
            device_id={"layer": across}, device_id_type=MESH,
        ).start()

    stages = ((0, relay_rows), (1, relay_flip), (5, relay_far), (6, share_last))
    score_behind = (6, 7)

    @pl.loop(0, pieces + score_behind[1])
    def _(step):
        @pl.when(step == 2)
        def _():
            own(3 + step * 0)

        for behind, stage in stages:
            pl.when((step >= behind) & (step < pieces + behind))(functools.partial(stage, step - behind))

        @pl.when(step >= score_behind[0])
        def _():
            valid = [(step >= behind) & (step < pieces + behind) for behind in score_behind]
            for part in range(2):
                pl.when(valid[part])(functools.partial(take, step - score_behind[part], part))
            both = product((q_hi[...], q_lo[...]), (t_hi[...], t_lo[...]))
            for part in (1, 0):
                pl.when(valid[part])(functools.partial(give, step - score_behind[part], part, both))

    by_way = [WAYS.count(way) for way in range(3)]
    sent = {3: by_way[0] + by_way[2], 4: by_way[1], 5: by_way[2], 6: by_way[0] + by_way[1]}
    for kind in [kind for kind in range(17) if kind not in (11, 12, 15, 16)]:
        block = held.at[pl.ds(0, 3 if kind in (10, 14) else 1), pl.ds(0, sent.get(kind, pieces) * ROWS), :]
        pltpu.make_async_copy(block, block, send_sem.at[kind]).wait()

    pl.loop(0, last)(gather_depth)
    pltpu.make_async_copy(crossed, crossed, cross_sem.at[1]).wait()

    @pl.loop(0, last)
    def _(piece):
        window = pl.ds(pl.multiple_of(piece * ROWS, ROWS), ROWS)
        mine = pl.ds(pl.multiple_of(kept * ROWS, ROWS), ROWS)
        o_ref[window, :] = (sums[piece, mine, :] + crossed[piece]) * weight[...]

    pltpu.make_async_copy(crossed, crossed, cross_sem.at[0]).wait()
    block = landed.at[:, pl.ds(0, depth - 1)]
    pltpu.make_async_copy(block, block, out_sem.at[0]).wait()
    block = direct.at[pl.ds(0, direct.shape[0] - 1)]
    pltpu.make_async_copy(block, block, out_sem.at[1]).wait()
    pltpu.make_async_copy(block, block, in_sem.at[last]).wait()
    o_ref[pl.ds(last * ROWS, ROWS), :] = jnp.sum(direct[...], axis=0) * weight[...]


def shards(query_grads, train_grads, eig_out, eig_in, eig_values, train_ids):
    query, train = query_grads[0], train_grads[0]
    count, flat = query.shape
    t_count = train.shape[0]
    layers = lax.axis_size("layer")
    everyone = lax.axis_size("dp") * count
    pieces = count // ROWS
    side = eig_out.shape[1]
    f32, bf16 = jnp.float32, jnp.bfloat16
    vmem = pl.BlockSpec(memory_space=pltpu.VMEM)
    return pl.pallas_call(
        kernel,
        out_shape=jax.ShapeDtypeStruct((count, t_count), f32),
        in_specs=[pl.BlockSpec(memory_space=pl.ANY)] * 6,
        out_specs=vmem,
        scratch_shapes=[
            pltpu.VMEM(eig_out.shape[1:], f32),
            pltpu.VMEM(eig_in.shape[1:], f32),
            pltpu.VMEM(eig_values.shape, f32),
            pltpu.VMEM((1, t_count), jnp.int32),
            pltpu.SemaphoreType.DMA((4,)),
            pltpu.VMEM((16, count, flat), f32),
            pltpu.VMEM((count, flat), f32),
            pltpu.VMEM((1, t_count), f32),
            pltpu.VMEM((t_count, flat), f32),
            pltpu.VMEM((flat, t_count), bf16),
            pltpu.VMEM((flat, t_count), bf16),
            pltpu.VMEM((16 * ROWS, flat), bf16),
            pltpu.VMEM((16 * ROWS, flat), bf16),
            pltpu.VMEM((side * ROWS, side * ROWS), bf16),
            pltpu.VMEM((side * ROWS, side * ROWS), bf16),
            pltpu.VMEM((side * PACK, side * PACK), bf16),
            pltpu.VMEM((side * PACK, side * PACK), bf16),
            pltpu.VMEM((side, side * ROWS), f32),
            pltpu.VMEM((pieces, 2, 8 * ROWS, t_count), f32),
            pltpu.VMEM((pieces - 1, layers // 2, 2 * ROWS, t_count), f32),
            pltpu.VMEM((layers, ROWS, t_count), f32),
            pltpu.VMEM((pieces - 1, 2 * ROWS, t_count), f32),
            pltpu.VMEM((pieces - 1, ROWS, t_count), f32),
            pltpu.SemaphoreType.DMA,
            pltpu.SemaphoreType.DMA,
            pltpu.SemaphoreType.DMA((17,)),
            pltpu.SemaphoreType.DMA((16, pieces)),
            pltpu.SemaphoreType.DMA((2,)),
            pltpu.SemaphoreType.DMA((pieces,)),
            pltpu.SemaphoreType.DMA((2,)),
        ],
        compiler_params=pltpu.CompilerParams(
            collective_id=0, has_side_effects=True, vmem_limit_bytes=56 * 1024 * 1024
        ),
        cost_estimate=pl.CostEstimate(
            flops=6 * everyone * t_count * flat, bytes_accessed=4 * flat * (count + t_count), transcendentals=0
        ),
    )(query, train, eig_out[0], eig_in[0], eig_values, train_ids[None])


def solution(mesh):
    placed = (
        P("layer", "dp", None),
        P("layer", "dp", None),
        P("layer", None, None),
        P("layer", None, None),
        P("layer", None),
        P("dp"),
    )
    return jax.shard_map(
        shards, mesh=mesh, in_specs=placed, out_specs=P("layer", "dp"), check_vma=False
    )
```

```python
import functools
import math
import operator

import jax
import jax.numpy as jnp
from jax import lax
from jax.experimental import pallas as pl
from jax.experimental.pallas import tpu as pltpu
from jax.sharding import PartitionSpec as P

CORPUS = 10000000
MESH = pl.DeviceIdType.MESH
ROWS = 8
GROUP = 16
WAYS = (0, 1, 2, 1, 0, 2, 1, 0)
PACK = 4

STEPS = ((0, 0), (0, 1), (0, -1), (1, 0), (0, 2), (1, 1), (1, -1), (1, 2))


def split(value):
    high = value.astype(jnp.bfloat16)
    low = (value - high.astype(jnp.float32)).astype(jnp.bfloat16)
    return high, low


def product(left, right, flipped=False):
    dims = (((1,), (1 if flipped else 0,)), ((), ()))
    dot = functools.partial(lax.dot_general, dimension_numbers=dims, preferred_element_type=jnp.float32)
    return dot(left[0], right[1]) + dot(left[1], right[0]) + dot(left[0], right[0])


def stack(flat):
    wide = PACK * 64
    return jnp.concatenate([flat[:, wide * i:wide * (i + 1)] for i in range(flat.shape[1] // wide)], axis=0)


def unstack(stacked):
    return jnp.concatenate([stacked[ROWS * i:ROWS * (i + 1), :] for i in range(stacked.shape[0] // ROWS)], axis=1)


def to_columns(stacked):
    turned = stacked.T
    side = turned.shape[0] // PACK
    return jnp.concatenate([turned[side * j:side * (j + 1), :] for j in range(PACK)], axis=1)


def from_columns(columns):
    wide = columns.shape[1] // PACK
    return jnp.concatenate([columns[:, wide * j:wide * (j + 1)] for j in range(PACK)], axis=0).T


def spread(basis, size, index, lane):
    side = basis.shape[0]
    iota = functools.partial(lax.broadcasted_iota, jnp.int32)
    tall = (index(iota((size, side), 0)) == iota((size, side), 1)).astype(jnp.bfloat16)
    wide = (iota((side, size), 0) == index(iota((side, size), 1))).astype(jnp.bfloat16)
    same = lane(iota((size, size), 0)) == lane(iota((size, size), 1))
    dot = functools.partial(jnp.dot, preferred_element_type=jnp.float32)
    return [
        jnp.where(same, dot(dot(tall, part).astype(jnp.bfloat16), wide), 0.0).astype(jnp.bfloat16)
        for part in split(basis)
    ]


def rotate(grads, out_op, in_op, inverse):
    parts = grads.shape[0] // ROWS
    tall = stack(grads[:ROWS]).shape[0]

    def each(turn, value, size):
        return jnp.concatenate([turn(value[size * k:size * (k + 1)]) for k in range(parts)], axis=0)

    value = each(stack, grads, ROWS)
    value = product(split(value), in_op)
    value = each(to_columns, value, tall)
    value = product(split(value), out_op)
    value = value * jnp.concatenate([inverse] * parts, axis=0)
    value = product(split(value), out_op, True)
    value = each(from_columns, value, 64)
    value = product(split(value), in_op, True)
    return each(unstack, value, tall)


def kernel(q_ref, t_ref, eig_out_hbm, eig_in_hbm, values_hbm, ids_hbm, o_ref,
           eig_out_ref, eig_in_ref, values_ref, ids_ref, small_sem,
           held, q_land, weight, t_land, t_hi, t_lo, q_hi, q_lo, out_hi, out_lo, in_hi, in_lo, inverse,
           scores, landed, direct, sums, crossed, load_sem, t_sem, send_sem, recv_sem, out_sem, in_sem, cross_sem):
    layer = lax.axis_index("layer")
    dp = lax.axis_index("dp")
    core, y, x = dp % 2, (dp // 2) % 4, dp // 8
    z, side = layer // 2, layer % 2
    count = q_ref.shape[0]
    pieces = count // ROWS
    depth = landed.shape[1]
    last = pieces - 1
    layers = direct.shape[0]

    def place(dx, dy, dc):
        return (((x + dx) % 2) * 4 + (y + dy + 4) % 4) * 2 + (core + dc) % 2

    x_flip, y_up, y_down, twin = place(1, 0, 0), place(0, 1, 0), place(0, -1, 0), place(0, 0, 1)
    across = z * 2 + 1 - side

    barrier = pltpu.get_barrier_semaphore()
    for other in (x_flip, y_up, y_down, twin):
        pl.semaphore_signal(barrier, inc=1, device_id={"dp": other}, device_id_type=MESH)

    @pl.loop(1, layers)
    def _(step):
        pl.semaphore_signal(barrier, inc=1, device_id={"layer": (layer + step) % layers}, device_id_type=MESH)

    small = [
        pltpu.make_async_copy(source, target, small_sem.at[at])
        for at, (source, target) in enumerate((
            (eig_out_hbm, eig_out_ref), (eig_in_hbm, eig_in_ref), (values_hbm, values_ref), (ids_hbm, ids_ref)
        ))
    ]
    for copy in small:
        copy.start()
    load = pltpu.make_async_copy(q_ref, q_land, load_sem)
    load.start()
    t_load = pltpu.make_async_copy(t_ref, t_land, t_sem)

    def send(slot, piece, target, to_slot, kind):
        window = pl.ds(pl.multiple_of(piece * ROWS, ROWS), ROWS)
        pltpu.make_async_remote_copy(
            src_ref=held.at[slot, window, :],
            dst_ref=held.at[to_slot, window, :],
            send_sem=send_sem.at[kind],
            recv_sem=recv_sem.at[to_slot, piece],
            device_id={"dp": target},
            device_id_type=MESH,
        ).start()

    def to_twin(slot, piece, slots=1, span=1):
        window = pl.ds(pl.multiple_of(piece * ROWS, ROWS), span * ROWS)
        pltpu.make_async_remote_copy(
            src_ref=held.at[pl.ds(slot, slots), window, :],
            dst_ref=held.at[pl.ds(8 + slot, slots), window, :],
            send_sem=send_sem.at[9 + slot],
            recv_sem=recv_sem.at[8 + slot, piece],
            device_id={"dp": twin},
            device_id_type=MESH,
        ).start()

    def arrive(slot, piece, slots=1, span=1):
        block = held.at[pl.ds(slot, slots), pl.ds(pl.multiple_of(piece * ROWS, ROWS), span * ROWS), :]
        pltpu.make_async_copy(block, block, recv_sem.at[slot, piece]).wait()

    for copy in small:
        copy.wait()
    out_hi[...], out_lo[...] = spread(
        eig_out_ref[...], out_hi.shape[0], lambda a: (a % 128) // ROWS * PACK + a // 128, lambda a: a % ROWS
    )
    in_hi[...], in_lo[...] = spread(eig_in_ref[...], in_hi.shape[0], lambda a: a % 64, lambda a: a // 64)
    values = values_ref[...]
    damped = 1.0 / (values + 0.1 * jnp.mean(values))
    inverse[...] = to_columns(stack(jnp.broadcast_to(damped, (ROWS, damped.shape[1]))))

    load.wait()
    t_load.start()

    def own(group):
        window = pl.ds(pl.multiple_of(group * GROUP, GROUP), GROUP)
        held[0, window, :] = rotate(
            q_land[window, :], (out_hi[...], out_lo[...]), (in_hi[...], in_lo[...]), inverse[...]
        )

        @pl.when(group == 0)
        def _():
            pl.semaphore_wait(barrier, 4 + layers - 1)

        for k in range(GROUP // ROWS):
            piece = group * (GROUP // ROWS) + k
            send(0, piece, y_up, 1, 0)
            send(0, piece, y_down, 2, 1)
            send(0, piece, x_flip, 3, 2)

        to_twin(0, group * (GROUP // ROWS), 1, GROUP // ROWS)

    pl.loop(0, 3)(own)

    position = ids_ref[...].astype(jnp.float32) / float(CORPUS)
    rate = 0.1 + 0.45 * (1.0 + jnp.cos(jnp.pi * position))
    weight[...] = rate / math.sqrt(float(q_ref.shape[1] * landed.shape[1] * 2))

    t_load.wait()
    t_count = t_ref.shape[0]

    @pl.loop(0, t_ref.shape[1] // t_count)
    def _(tile):
        window = pl.ds(pl.multiple_of(tile * t_count, t_count), t_count)
        t_hi[window, :], t_lo[window, :] = split(t_land[:, window].T)

    def goes(piece, way):
        return functools.reduce(operator.or_, [piece == at for at in range(pieces) if WAYS[at] == way])

    def relay_rows(piece):
        arrive(1, piece)

        @pl.when(jnp.logical_not(goes(piece, 1)))
        def _():
            send(1, piece, y_up, 4, 3)

        @pl.when(goes(piece, 2))
        def _():
            send(1, piece, x_flip, 5, 5)

        arrive(2, piece)

        @pl.when(goes(piece, 1))
        def _():
            send(2, piece, y_down, 4, 4)


    def relay_flip(piece):
        arrive(3, piece)

        @pl.when(jnp.logical_not(goes(piece, 2)))
        def _():
            send(3, piece, y_up, 5, 6)

        send(3, piece, y_down, 6, 7)

        @pl.when(piece % 2 == 1)
        def _():
            to_twin(1, piece - 1, 3, 2)

    def relay_far(piece):
        arrive(4, piece)
        send(4, piece, x_flip, 7, 8)
        to_twin(4, piece)

    def share_last(piece):
        arrive(7, piece)
        arrive(5, piece)
        arrive(6, piece)
        to_twin(5, piece, 3)

    def take(piece, part):
        window = pl.ds(pl.multiple_of(piece * ROWS, ROWS), ROWS)
        if part == 0:
            @pl.when(piece % 2 == 0)
            def _():
                arrive(8, piece, 1, 2)
                arrive(9, piece, 3, 2)
        else:
            arrive(12, piece)
            arrive(13, piece, 3)
        for at in range(4):
            slot = 4 * part + at
            to = pl.ds(slot * 2 * ROWS, 2 * ROWS)
            both = jnp.concatenate([held[slot, window, :], held[8 + slot, window, :]], axis=0)
            q_hi[to, :], q_lo[to, :] = split(both)

    def give(piece, part, both):
        scores[piece, part] = both[part * 8 * ROWS:(part + 1) * 8 * ROWS]
        slots = range(4 * part, 4 * part + 4)
        owners = [place(STEPS[slot][0], -STEPS[slot][1], 0) // 2 for slot in slots]

        @pl.when(piece < last)
        def _():
            for at, owner in enumerate(owners):
                block = pl.ds(at * 2 * ROWS, 2 * ROWS)

                @pl.when(owner != z)
                def _():
                    pltpu.make_async_remote_copy(
                        src_ref=scores.at[piece, part, block, :], dst_ref=landed.at[piece, z],
                        send_sem=out_sem.at[0], recv_sem=in_sem.at[piece],
                        device_id={"layer": owner * 2 + side}, device_id_type=MESH,
                    ).start()

                @pl.when(owner == z)
                def _():
                    landed[piece, z] = scores[piece, part, block, :]

        @pl.when(piece == last)
        def _():
            for at, owner in enumerate(owners):
                for other in range(2):
                    target = owner * 2 + (core + other) % 2
                    block = pl.ds((at * 2 + other) * ROWS, ROWS)

                    @pl.when(target != layer)
                    def _():
                        pltpu.make_async_remote_copy(
                            src_ref=scores.at[last, part, block, :], dst_ref=direct.at[layer],
                            send_sem=out_sem.at[1], recv_sem=in_sem.at[last],
                            device_id={"layer": target}, device_id_type=MESH,
                        ).start()

                    @pl.when(target == layer)
                    def _():
                        direct[layer] = scores[last, part, block, :]

    kept = (core + side) % 2

    def gather_depth(piece):
        block = landed.at[piece, pl.ds(0, depth - 1)]
        pltpu.make_async_copy(block, block, in_sem.at[piece]).wait()
        sums[piece] = jnp.sum(landed[piece], axis=0)
        pltpu.make_async_remote_copy(
            src_ref=sums.at[piece, pl.ds(pl.multiple_of((1 - kept) * ROWS, ROWS), ROWS), :],
            dst_ref=crossed.at[piece],
            send_sem=cross_sem.at[0], recv_sem=cross_sem.at[1],
            device_id={"layer": across}, device_id_type=MESH,
        ).start()

    stages = ((0, relay_rows), (1, relay_flip), (4, relay_far), (6, share_last))
    score_behind = (6, 7)

    @pl.loop(0, pieces + score_behind[1])
    def _(step):
        @pl.when(step == 2)
        def _():
            own(3 + step * 0)

        for behind, stage in stages:
            pl.when((step >= behind) & (step < pieces + behind))(functools.partial(stage, step - behind))

        @pl.when(step >= score_behind[0])
        def _():
            valid = [(step >= behind) & (step < pieces + behind) for behind in score_behind]
            for part in range(2):
                pl.when(valid[part])(functools.partial(take, step - score_behind[part], part))
            both = product((q_hi[...], q_lo[...]), (t_hi[...], t_lo[...]))
            for part in (1, 0):
                pl.when(valid[part])(functools.partial(give, step - score_behind[part], part, both))

    by_way = [WAYS.count(way) for way in range(3)]
    sent = {3: by_way[0] + by_way[2], 4: by_way[1], 5: by_way[2], 6: by_way[0] + by_way[1]}
    for kind in [kind for kind in range(17) if kind not in (11, 12, 15, 16)]:
        block = held.at[pl.ds(0, 3 if kind in (10, 14) else 1), pl.ds(0, sent.get(kind, pieces) * ROWS), :]
        pltpu.make_async_copy(block, block, send_sem.at[kind]).wait()

    pl.loop(0, last)(gather_depth)
    pltpu.make_async_copy(crossed, crossed, cross_sem.at[1]).wait()

    @pl.loop(0, last)
    def _(piece):
        window = pl.ds(pl.multiple_of(piece * ROWS, ROWS), ROWS)
        mine = pl.ds(pl.multiple_of(kept * ROWS, ROWS), ROWS)
        o_ref[window, :] = (sums[piece, mine, :] + crossed[piece]) * weight[...]

    pltpu.make_async_copy(crossed, crossed, cross_sem.at[0]).wait()
    block = landed.at[:, pl.ds(0, depth - 1)]
    pltpu.make_async_copy(block, block, out_sem.at[0]).wait()
    block = direct.at[pl.ds(0, direct.shape[0] - 1)]
    pltpu.make_async_copy(block, block, out_sem.at[1]).wait()
    pltpu.make_async_copy(block, block, in_sem.at[last]).wait()
    o_ref[pl.ds(last * ROWS, ROWS), :] = jnp.sum(direct[...], axis=0) * weight[...]


def shards(query_grads, train_grads, eig_out, eig_in, eig_values, train_ids):
    query, train = query_grads[0], train_grads[0]
    count, flat = query.shape
    t_count = train.shape[0]
    layers = lax.axis_size("layer")
    everyone = lax.axis_size("dp") * count
    pieces = count // ROWS
    side = eig_out.shape[1]
    f32, bf16 = jnp.float32, jnp.bfloat16
    vmem = pl.BlockSpec(memory_space=pltpu.VMEM)
    return pl.pallas_call(
        kernel,
        out_shape=jax.ShapeDtypeStruct((count, t_count), f32),
        in_specs=[pl.BlockSpec(memory_space=pl.ANY)] * 6,
        out_specs=vmem,
        scratch_shapes=[
            pltpu.VMEM(eig_out.shape[1:], f32),
            pltpu.VMEM(eig_in.shape[1:], f32),
            pltpu.VMEM(eig_values.shape, f32),
            pltpu.VMEM((1, t_count), jnp.int32),
            pltpu.SemaphoreType.DMA((4,)),
            pltpu.VMEM((16, count, flat), f32),
            pltpu.VMEM((count, flat), f32),
            pltpu.VMEM((1, t_count), f32),
            pltpu.VMEM((t_count, flat), f32),
            pltpu.VMEM((flat, t_count), bf16),
            pltpu.VMEM((flat, t_count), bf16),
            pltpu.VMEM((16 * ROWS, flat), bf16),
            pltpu.VMEM((16 * ROWS, flat), bf16),
            pltpu.VMEM((side * ROWS, side * ROWS), bf16),
            pltpu.VMEM((side * ROWS, side * ROWS), bf16),
            pltpu.VMEM((side * PACK, side * PACK), bf16),
            pltpu.VMEM((side * PACK, side * PACK), bf16),
            pltpu.VMEM((side, side * ROWS), f32),
            pltpu.VMEM((pieces, 2, 8 * ROWS, t_count), f32),
            pltpu.VMEM((pieces - 1, layers // 2, 2 * ROWS, t_count), f32),
            pltpu.VMEM((layers, ROWS, t_count), f32),
            pltpu.VMEM((pieces - 1, 2 * ROWS, t_count), f32),
            pltpu.VMEM((pieces - 1, ROWS, t_count), f32),
            pltpu.SemaphoreType.DMA,
            pltpu.SemaphoreType.DMA,
            pltpu.SemaphoreType.DMA((17,)),
            pltpu.SemaphoreType.DMA((16, pieces)),
            pltpu.SemaphoreType.DMA((2,)),
            pltpu.SemaphoreType.DMA((pieces,)),
            pltpu.SemaphoreType.DMA((2,)),
        ],
        compiler_params=pltpu.CompilerParams(
            collective_id=0, has_side_effects=True, vmem_limit_bytes=56 * 1024 * 1024
        ),
        cost_estimate=pl.CostEstimate(
            flops=6 * everyone * t_count * flat, bytes_accessed=4 * flat * (count + t_count), transcendentals=0
        ),
    )(query, train, eig_out[0], eig_in[0], eig_values, train_ids[None])


def solution(mesh):
    placed = (
        P("layer", "dp", None),
        P("layer", "dp", None),
        P("layer", None, None),
        P("layer", None, None),
        P("layer", None),
        P("dp"),
    )
    return jax.shard_map(
        shards, mesh=mesh, in_specs=placed, out_specs=P("layer", "dp"), check_vma=False
    )
```

```python
import functools
import math
import operator

import jax
import jax.numpy as jnp
from jax import lax
from jax.experimental import pallas as pl
from jax.experimental.pallas import tpu as pltpu
from jax.sharding import PartitionSpec as P

CORPUS = 10000000
MESH = pl.DeviceIdType.MESH
ROWS = 8
GROUP = 16
WAYS = (0, 1, 2, 1, 0, 2, 1, 0)
PACK = 4

STEPS = ((0, 0), (0, 1), (0, -1), (1, 0), (0, 2), (1, 1), (1, -1), (1, 2))


def split(value):
    high = value.astype(jnp.bfloat16)
    low = (value - high.astype(jnp.float32)).astype(jnp.bfloat16)
    return high, low


def product(left, right, flipped=False):
    dims = (((1,), (1 if flipped else 0,)), ((), ()))
    dot = functools.partial(lax.dot_general, dimension_numbers=dims, preferred_element_type=jnp.float32)
    return dot(left[0], right[1]) + dot(left[1], right[0]) + dot(left[0], right[0])


def stack(flat):
    wide = PACK * 64
    return jnp.concatenate([flat[:, wide * i:wide * (i + 1)] for i in range(flat.shape[1] // wide)], axis=0)


def unstack(stacked):
    return jnp.concatenate([stacked[ROWS * i:ROWS * (i + 1), :] for i in range(stacked.shape[0] // ROWS)], axis=1)


def to_columns(stacked):
    turned = stacked.T
    side = turned.shape[0] // PACK
    return jnp.concatenate([turned[side * j:side * (j + 1), :] for j in range(PACK)], axis=1)


def from_columns(columns):
    wide = columns.shape[1] // PACK
    return jnp.concatenate([columns[:, wide * j:wide * (j + 1)] for j in range(PACK)], axis=0).T


def spread(basis, size, index, lane):
    side = basis.shape[0]
    iota = functools.partial(lax.broadcasted_iota, jnp.int32)
    tall = (index(iota((size, side), 0)) == iota((size, side), 1)).astype(jnp.bfloat16)
    wide = (iota((side, size), 0) == index(iota((side, size), 1))).astype(jnp.bfloat16)
    same = lane(iota((size, size), 0)) == lane(iota((size, size), 1))
    dot = functools.partial(jnp.dot, preferred_element_type=jnp.float32)
    return [
        jnp.where(same, dot(dot(tall, part).astype(jnp.bfloat16), wide), 0.0).astype(jnp.bfloat16)
        for part in split(basis)
    ]


def rotate(grads, out_op, in_op, inverse):
    parts = grads.shape[0] // ROWS
    tall = stack(grads[:ROWS]).shape[0]

    def each(turn, value, size):
        return jnp.concatenate([turn(value[size * k:size * (k + 1)]) for k in range(parts)], axis=0)

    value = each(stack, grads, ROWS)
    value = product(split(value), in_op)
    value = each(to_columns, value, tall)
    value = product(split(value), out_op)
    value = value * jnp.concatenate([inverse] * parts, axis=0)
    value = product(split(value), out_op, True)
    value = each(from_columns, value, 64)
    value = product(split(value), in_op, True)
    return each(unstack, value, tall)


def kernel(q_ref, t_ref, eig_out_hbm, eig_in_hbm, values_hbm, ids_hbm, o_ref,
           eig_out_ref, eig_in_ref, values_ref, ids_ref, small_sem,
           held, q_land, weight, t_land, t_hi, t_lo, q_hi, q_lo, out_hi, out_lo, in_hi, in_lo, inverse,
           scores, landed, direct, sums, crossed, load_sem, t_sem, send_sem, recv_sem, out_sem, in_sem, cross_sem):
    layer = lax.axis_index("layer")
    dp = lax.axis_index("dp")
    core, y, x = dp % 2, (dp // 2) % 4, dp // 8
    z, side = layer // 2, layer % 2
    count = q_ref.shape[0]
    pieces = count // ROWS
    depth = landed.shape[1]
    last = pieces - 1
    layers = direct.shape[0]

    def place(dx, dy, dc):
        return (((x + dx) % 2) * 4 + (y + dy + 4) % 4) * 2 + (core + dc) % 2

    x_flip, y_up, y_down, twin = place(1, 0, 0), place(0, 1, 0), place(0, -1, 0), place(0, 0, 1)
    across = z * 2 + 1 - side

    barrier = pltpu.get_barrier_semaphore()
    for other in (x_flip, y_up, y_down, twin):
        pl.semaphore_signal(barrier, inc=1, device_id={"dp": other}, device_id_type=MESH)

    @pl.loop(1, layers)
    def _(step):
        pl.semaphore_signal(barrier, inc=1, device_id={"layer": (layer + step) % layers}, device_id_type=MESH)

    small = [
        pltpu.make_async_copy(source, target, small_sem.at[at])
        for at, (source, target) in enumerate((
            (eig_out_hbm, eig_out_ref), (eig_in_hbm, eig_in_ref), (values_hbm, values_ref), (ids_hbm, ids_ref)
        ))
    ]
    for copy in small:
        copy.start()
    load = pltpu.make_async_copy(q_ref, q_land, load_sem)
    load.start()
    t_load = pltpu.make_async_copy(t_ref, t_land, t_sem)

    def send(slot, piece, target, to_slot, kind):
        window = pl.ds(pl.multiple_of(piece * ROWS, ROWS), ROWS)
        pltpu.make_async_remote_copy(
            src_ref=held.at[slot, window, :],
            dst_ref=held.at[to_slot, window, :],
            send_sem=send_sem.at[kind],
            recv_sem=recv_sem.at[to_slot, piece],
            device_id={"dp": target},
            device_id_type=MESH,
        ).start()

    def to_twin(slot, piece, slots=1, span=1):
        window = pl.ds(pl.multiple_of(piece * ROWS, ROWS), span * ROWS)
        pltpu.make_async_remote_copy(
            src_ref=held.at[pl.ds(slot, slots), window, :],
            dst_ref=held.at[pl.ds(8 + slot, slots), window, :],
            send_sem=send_sem.at[9 + slot],
            recv_sem=recv_sem.at[8 + slot, piece],
            device_id={"dp": twin},
            device_id_type=MESH,
        ).start()

    def arrive(slot, piece, slots=1, span=1):
        block = held.at[pl.ds(slot, slots), pl.ds(pl.multiple_of(piece * ROWS, ROWS), span * ROWS), :]
        pltpu.make_async_copy(block, block, recv_sem.at[slot, piece]).wait()

    for copy in small:
        copy.wait()
    out_hi[...], out_lo[...] = spread(
        eig_out_ref[...], out_hi.shape[0], lambda a: (a % 128) // ROWS * PACK + a // 128, lambda a: a % ROWS
    )
    in_hi[...], in_lo[...] = spread(eig_in_ref[...], in_hi.shape[0], lambda a: a % 64, lambda a: a // 64)
    values = values_ref[...]
    damped = 1.0 / (values + 0.1 * jnp.mean(values))
    inverse[...] = to_columns(stack(jnp.broadcast_to(damped, (ROWS, damped.shape[1]))))

    load.wait()
    t_load.start()

    def own(group):
        window = pl.ds(pl.multiple_of(group * GROUP, GROUP), GROUP)
        held[0, window, :] = rotate(
            q_land[window, :], (out_hi[...], out_lo[...]), (in_hi[...], in_lo[...]), inverse[...]
        )

        @pl.when(group == 0)
        def _():
            pl.semaphore_wait(barrier, 4 + layers - 1)

        for k in range(GROUP // ROWS):
            piece = group * (GROUP // ROWS) + k
            send(0, piece, y_up, 1, 0)
            send(0, piece, y_down, 2, 1)
            send(0, piece, x_flip, 3, 2)

        to_twin(0, group * (GROUP // ROWS), 1, GROUP // ROWS)

    pl.loop(0, 3)(own)

    position = ids_ref[...].astype(jnp.float32) / float(CORPUS)
    rate = 0.1 + 0.45 * (1.0 + jnp.cos(jnp.pi * position))
    weight[...] = rate / math.sqrt(float(q_ref.shape[1] * landed.shape[1] * 2))

    def turn_train():
        t_load.wait()
        t_count = t_ref.shape[0]

        @pl.loop(0, t_ref.shape[1] // t_count)
        def _(tile):
            window = pl.ds(pl.multiple_of(tile * t_count, t_count), t_count)
            t_hi[window, :], t_lo[window, :] = split(t_land[:, window].T)

    def goes(piece, way):
        return functools.reduce(operator.or_, [piece == at for at in range(pieces) if WAYS[at] == way])

    def relay_rows(piece):
        arrive(1, piece)

        @pl.when(jnp.logical_not(goes(piece, 1)))
        def _():
            send(1, piece, y_up, 4, 3)

        @pl.when(goes(piece, 2))
        def _():
            send(1, piece, x_flip, 5, 5)

        arrive(2, piece)

        @pl.when(goes(piece, 1))
        def _():
            send(2, piece, y_down, 4, 4)


    def relay_flip(piece):
        arrive(3, piece)

        @pl.when(jnp.logical_not(goes(piece, 2)))
        def _():
            send(3, piece, y_up, 5, 6)

        send(3, piece, y_down, 6, 7)

        @pl.when(piece % 2 == 1)
        def _():
            to_twin(1, piece - 1, 3, 2)

    def relay_far(piece):
        arrive(4, piece)
        send(4, piece, x_flip, 7, 8)
        to_twin(4, piece)

    def share_last(piece):
        arrive(7, piece)
        arrive(5, piece)
        arrive(6, piece)
        to_twin(5, piece, 3)

    def take(piece, part):
        window = pl.ds(pl.multiple_of(piece * ROWS, ROWS), ROWS)
        if part == 0:
            @pl.when(piece % 2 == 0)
            def _():
                arrive(8, piece, 1, 2)
                arrive(9, piece, 3, 2)
        else:
            arrive(12, piece)
            arrive(13, piece, 3)
        for at in range(4):
            slot = 4 * part + at
            to = pl.ds(slot * 2 * ROWS, 2 * ROWS)
            both = jnp.concatenate([held[slot, window, :], held[8 + slot, window, :]], axis=0)
            q_hi[to, :], q_lo[to, :] = split(both)

    def give(piece, part, both):
        scores[piece, part] = both[part * 8 * ROWS:(part + 1) * 8 * ROWS]
        slots = range(4 * part, 4 * part + 4)
        owners = [place(STEPS[slot][0], -STEPS[slot][1], 0) // 2 for slot in slots]

        @pl.when(piece < last)
        def _():
            for at, owner in enumerate(owners):
                block = pl.ds(at * 2 * ROWS, 2 * ROWS)

                @pl.when(owner != z)
                def _():
                    pltpu.make_async_remote_copy(
                        src_ref=scores.at[piece, part, block, :], dst_ref=landed.at[piece, z],
                        send_sem=out_sem.at[0], recv_sem=in_sem.at[piece],
                        device_id={"layer": owner * 2 + side}, device_id_type=MESH,
                    ).start()

                @pl.when(owner == z)
                def _():
                    landed[piece, z] = scores[piece, part, block, :]

        @pl.when(piece == last)
        def _():
            for at, owner in enumerate(owners):
                for other in range(2):
                    target = owner * 2 + (core + other) % 2
                    block = pl.ds((at * 2 + other) * ROWS, ROWS)

                    @pl.when(target != layer)
                    def _():
                        pltpu.make_async_remote_copy(
                            src_ref=scores.at[last, part, block, :], dst_ref=direct.at[layer],
                            send_sem=out_sem.at[1], recv_sem=in_sem.at[last],
                            device_id={"layer": target}, device_id_type=MESH,
                        ).start()

                    @pl.when(target == layer)
                    def _():
                        direct[layer] = scores[last, part, block, :]

    kept = (core + side) % 2

    def gather_depth(piece):
        block = landed.at[piece, pl.ds(0, depth - 1)]
        pltpu.make_async_copy(block, block, in_sem.at[piece]).wait()
        sums[piece] = jnp.sum(landed[piece], axis=0)
        pltpu.make_async_remote_copy(
            src_ref=sums.at[piece, pl.ds(pl.multiple_of((1 - kept) * ROWS, ROWS), ROWS), :],
            dst_ref=crossed.at[piece],
            send_sem=cross_sem.at[0], recv_sem=cross_sem.at[1],
            device_id={"layer": across}, device_id_type=MESH,
        ).start()

    stages = ((0, relay_rows), (1, relay_flip), (4, relay_far), (6, share_last))
    score_behind = (6, 7)

    @pl.loop(0, pieces + score_behind[1])
    def _(step):
        @pl.when(step == 2)
        def _():
            own(3 + step * 0)

        pl.when(step == 3)(turn_train)

        for behind, stage in stages:
            pl.when((step >= behind) & (step < pieces + behind))(functools.partial(stage, step - behind))

        @pl.when(step >= score_behind[0])
        def _():
            valid = [(step >= behind) & (step < pieces + behind) for behind in score_behind]
            for part in range(2):
                pl.when(valid[part])(functools.partial(take, step - score_behind[part], part))
            both = product((q_hi[...], q_lo[...]), (t_hi[...], t_lo[...]))
            for part in (1, 0):
                pl.when(valid[part])(functools.partial(give, step - score_behind[part], part, both))

    by_way = [WAYS.count(way) for way in range(3)]
    sent = {3: by_way[0] + by_way[2], 4: by_way[1], 5: by_way[2], 6: by_way[0] + by_way[1]}
    for kind in [kind for kind in range(17) if kind not in (11, 12, 15, 16)]:
        block = held.at[pl.ds(0, 3 if kind in (10, 14) else 1), pl.ds(0, sent.get(kind, pieces) * ROWS), :]
        pltpu.make_async_copy(block, block, send_sem.at[kind]).wait()

    pl.loop(0, last)(gather_depth)
    pltpu.make_async_copy(crossed, crossed, cross_sem.at[1]).wait()

    @pl.loop(0, last)
    def _(piece):
        window = pl.ds(pl.multiple_of(piece * ROWS, ROWS), ROWS)
        mine = pl.ds(pl.multiple_of(kept * ROWS, ROWS), ROWS)
        o_ref[window, :] = (sums[piece, mine, :] + crossed[piece]) * weight[...]

    pltpu.make_async_copy(crossed, crossed, cross_sem.at[0]).wait()
    block = landed.at[:, pl.ds(0, depth - 1)]
    pltpu.make_async_copy(block, block, out_sem.at[0]).wait()
    block = direct.at[pl.ds(0, direct.shape[0] - 1)]
    pltpu.make_async_copy(block, block, out_sem.at[1]).wait()
    pltpu.make_async_copy(block, block, in_sem.at[last]).wait()
    o_ref[pl.ds(last * ROWS, ROWS), :] = jnp.sum(direct[...], axis=0) * weight[...]


def shards(query_grads, train_grads, eig_out, eig_in, eig_values, train_ids):
    query, train = query_grads[0], train_grads[0]
    count, flat = query.shape
    t_count = train.shape[0]
    layers = lax.axis_size("layer")
    everyone = lax.axis_size("dp") * count
    pieces = count // ROWS
    side = eig_out.shape[1]
    f32, bf16 = jnp.float32, jnp.bfloat16
    vmem = pl.BlockSpec(memory_space=pltpu.VMEM)
    return pl.pallas_call(
        kernel,
        out_shape=jax.ShapeDtypeStruct((count, t_count), f32),
        in_specs=[pl.BlockSpec(memory_space=pl.ANY)] * 6,
        out_specs=vmem,
        scratch_shapes=[
            pltpu.VMEM(eig_out.shape[1:], f32),
            pltpu.VMEM(eig_in.shape[1:], f32),
            pltpu.VMEM(eig_values.shape, f32),
            pltpu.VMEM((1, t_count), jnp.int32),
            pltpu.SemaphoreType.DMA((4,)),
            pltpu.VMEM((16, count, flat), f32),
            pltpu.VMEM((count, flat), f32),
            pltpu.VMEM((1, t_count), f32),
            pltpu.VMEM((t_count, flat), f32),
            pltpu.VMEM((flat, t_count), bf16),
            pltpu.VMEM((flat, t_count), bf16),
            pltpu.VMEM((16 * ROWS, flat), bf16),
            pltpu.VMEM((16 * ROWS, flat), bf16),
            pltpu.VMEM((side * ROWS, side * ROWS), bf16),
            pltpu.VMEM((side * ROWS, side * ROWS), bf16),
            pltpu.VMEM((side * PACK, side * PACK), bf16),
            pltpu.VMEM((side * PACK, side * PACK), bf16),
            pltpu.VMEM((side, side * ROWS), f32),
            pltpu.VMEM((pieces, 2, 8 * ROWS, t_count), f32),
            pltpu.VMEM((pieces - 1, layers // 2, 2 * ROWS, t_count), f32),
            pltpu.VMEM((layers, ROWS, t_count), f32),
            pltpu.VMEM((pieces - 1, 2 * ROWS, t_count), f32),
            pltpu.VMEM((pieces - 1, ROWS, t_count), f32),
            pltpu.SemaphoreType.DMA,
            pltpu.SemaphoreType.DMA,
            pltpu.SemaphoreType.DMA((17,)),
            pltpu.SemaphoreType.DMA((16, pieces)),
            pltpu.SemaphoreType.DMA((2,)),
            pltpu.SemaphoreType.DMA((pieces,)),
            pltpu.SemaphoreType.DMA((2,)),
        ],
        compiler_params=pltpu.CompilerParams(
            collective_id=0, has_side_effects=True, vmem_limit_bytes=56 * 1024 * 1024
        ),
        cost_estimate=pl.CostEstimate(
            flops=6 * everyone * t_count * flat, bytes_accessed=4 * flat * (count + t_count), transcendentals=0
        ),
    )(query, train, eig_out[0], eig_in[0], eig_values, train_ids[None])


def solution(mesh):
    placed = (
        P("layer", "dp", None),
        P("layer", "dp", None),
        P("layer", None, None),
        P("layer", None, None),
        P("layer", None),
        P("dp"),
    )
    return jax.shard_map(
        shards, mesh=mesh, in_specs=placed, out_specs=P("layer", "dp"), check_vma=False
    )
```
